32 devices in a mesh: peer: 16 (over z, y, core), grp: 2 (over x).
Axes of the slice: x: 2, y: 2, z: 4, core: 2. Of those that a mesh axis runs over, the one named last changes fastest.
Arguments:
- images: bfloat16 [2, 16, 2, 8, 32, 384], P(None, 'peer', 'grp'), may hold values from -6 to 6
- cotangent: bfloat16 [2, 16, 2, 8, 32, 384], P(None, 'peer', 'grp'), may hold values from -6 to 6
- dw_kernel: float32 [16, 49, 384], P('peer', None, 'grp'), may hold values from -0.875 to 0.875
- chan_vec: float32 [16, 5, 384], P('peer', None, 'grp'), may hold values from 0.25 to 1.5
- w_in: float32 [16, 384, 1536], P('peer', 'grp'), may hold values from -0.3125 to 0.3125
- b_in: float32 [16, 1536], P('peer', 'grp'), may hold values from -3 to 3
- w_out: float32 [16, 1536, 384], P('peer', 'grp'), may hold values from -0.15625 to 0.15625
- mom_kernel: float32 [16, 49, 384], P('peer', None, 'grp'), may hold values from -300 to 300
- mom_chan: float32 [16, 5, 384], P('peer', None, 'grp'), may hold values from -300 to 300
- mom_in: float32 [16, 384, 1536], P('peer', 'grp'), may hold values from -300 to 300
- mom_bin: float32 [16, 1536], P('peer', 'grp'), may hold values from -300 to 300
- mom_out: float32 [16, 1536, 384], P('peer', 'grp'), may hold values from -300 to 300
Outputs:
- new_kernel: float32 [16, 49, 384], P('peer', None, 'grp')
- new_chan: float32 [16, 5, 384], P('peer', None, 'grp')
- new_in: float32 [16, 384, 1536], P('peer', 'grp')
- new_bin: float32 [16, 1536], P('peer', 'grp')
- new_out: float32 [16, 1536, 384], P('peer', 'grp')
- features: bfloat16 [16, 2, 8, 32, 384], P('peer', 'grp')
The draws below stay inside these ranges and needn't reach their ends.
All inputs are finite; a program needn't handle non-finite values.
Results may differ from the reference program's by a relative error of at most 0.01.
Values may be sent and summed in bfloat16 or wider, within the bound.
A program may use at most 64 MiB of HBM per device.

```python
import math
import jax
import jax.numpy as jnp
from jax import lax

CHANNELS = 384
HIDDEN_SIZE = 1536
HEIGHT = 8
WIDTH = 32
TAPS = 49
STEPS = 2
REPLICAS = 16
GROUPS = 2


def block_scale(key, shape, shards, low, high):
    def one(axis_at, blocks):
        steps = jax.random.uniform(jax.random.fold_in(jax.random.fold_in(key, 6), axis_at), (blocks,), jnp.float32, low / len(shards), high / len(shards))
        return jnp.repeat(jnp.exp(steps), shape[axis_at] // blocks).reshape((-1,) + (1,) * (len(shape) - axis_at - 1))

    loudness = one(*shards[0])
    for cut in shards[1:]:
        loudness = loudness * one(*cut)
    return loudness


def centred(rng, dims, scale, most, cuts=(), held_as=jnp.bfloat16):
    result = jax.random.normal(rng, dims, jnp.float32) * scale
    if len(cuts) > 0:
        result = block_scale(rng, dims, cuts, -0.22, 0.18) * result
    return jnp.clip(result, min=-most, max=most).astype(held_as)


def setup_inputs(seed: int = 0) -> dict:
    arg_keys = jax.random.split(jax.random.key(seed), 13)
    return {
        "images": centred(arg_keys[0], (STEPS, REPLICAS, GROUPS, HEIGHT, WIDTH, CHANNELS), 1.0, 6.0, ((1, 16), (2, 2))),
        "cotangent": centred(arg_keys[1], (STEPS, REPLICAS, GROUPS, HEIGHT, WIDTH, CHANNELS), 1.0, 6.0, ((1, 16), (2, 2))),
        "dw_kernel": centred(arg_keys[2], (REPLICAS, TAPS, CHANNELS), TAPS ** -0.5, 0.875, ((0, 16), (2, 2)), jnp.float32),
        "chan_vec": jnp.clip(0.25 + 1.25 * jax.random.uniform(arg_keys[3], (REPLICAS, 5, CHANNELS), jnp.float32) ** block_scale(arg_keys[3], (REPLICAS, 5, CHANNELS), ((0, 16), (2, 2)), -0.2, 0.2), 0.25, 1.5),
        "w_in": centred(arg_keys[4], (REPLICAS, CHANNELS, HIDDEN_SIZE), CHANNELS ** -0.5, 0.3125, ((0, 16), (1, 2)), jnp.float32),
        "b_in": centred(arg_keys[5], (REPLICAS, HIDDEN_SIZE), 0.5, 3.0, ((0, 16), (1, 2)), jnp.float32),
        "w_out": centred(arg_keys[6], (REPLICAS, HIDDEN_SIZE, CHANNELS), HIDDEN_SIZE ** -0.5, 0.15625, ((0, 16), (1, 2)), jnp.float32),
        "mom_kernel": centred(arg_keys[7], (REPLICAS, TAPS, CHANNELS), 50.0, 300.0, ((0, 16), (2, 2)), jnp.float32),
        "mom_chan": centred(arg_keys[8], (REPLICAS, 5, CHANNELS), 50.0, 300.0, ((0, 16), (2, 2)), jnp.float32),
        "mom_in": centred(arg_keys[9], (REPLICAS, CHANNELS, HIDDEN_SIZE), 50.0, 300.0, ((0, 16), (1, 2)), jnp.float32),
        "mom_bin": centred(arg_keys[10], (REPLICAS, HIDDEN_SIZE), 50.0, 300.0, ((0, 16), (1, 2)), jnp.float32),
        "mom_out": centred(arg_keys[11], (REPLICAS, HIDDEN_SIZE, CHANNELS), 50.0, 300.0, ((0, 16), (1, 2)), jnp.float32),
    }


EPS = 1e-06
MOMENTUM = 0.9
RATE = 0.0005
SQRT_HALF = 0.7071067811865476
INV_ROOT_TWO_PI = 0.3989422804014327

def depthwise(field, kernel):
    channels = kernel.shape[-1]
    reach = math.isqrt(kernel.shape[0])
    margin = reach // 2
    filter_taps = kernel.reshape(reach, reach, 1, channels)
    return lax.conv_general_dilated(field, filter_taps, (1, 1), ((margin, margin), (margin, margin)), dimension_numbers=('NHWC', 'HWIO', 'NHWC'), feature_group_count=channels, precision=lax.Precision.HIGHEST)

def gelu_value(value):
    return 0.5 * value * (1.0 + lax.erf(value * SQRT_HALF))

def gelu_slope(value):
    return 0.5 * (1.0 + lax.erf(value * SQRT_HALF)) + value * jnp.exp(-0.5 * value * value) * INV_ROOT_TWO_PI

def channel_front(image, kernel, chan):
    height, width, channels = image.shape
    field = image.astype(jnp.float32)[None]
    conv = depthwise(field, kernel)[0].reshape(height * width, channels) + chan[0]
    center = conv - lax.optimization_barrier(jnp.mean(conv, axis=-1, keepdims=True))
    spread = lax.rsqrt(lax.optimization_barrier(jnp.mean(center * center, axis=-1, keepdims=True)) + EPS)
    scaled = center * spread
    normed = (scaled * chan[1] + chan[2]).astype(jnp.bfloat16)
    return (field, scaled, spread, normed)

def channel_back(field, scaled, spread, dnormed, chan, kernel, bias_grad, scale_grad):
    d_gain = lax.optimization_barrier(jnp.sum(dnormed * scaled, axis=0))
    d_shift = lax.optimization_barrier(jnp.sum(dnormed, axis=0))
    dscaled = dnormed * chan[1]
    dconv = spread * (dscaled - lax.optimization_barrier(jnp.mean(dscaled, axis=-1, keepdims=True)) - scaled * lax.optimization_barrier(jnp.mean(dscaled * scaled, axis=-1, keepdims=True)))
    d_bias = lax.optimization_barrier(jnp.sum(dconv, axis=0))
    _, pullback = jax.vjp(lambda taps: depthwise(field, taps), kernel)
    d_kernel, = pullback(dconv.reshape(field.shape))
    d_chan = jnp.stack([d_bias, d_gain, d_shift, bias_grad, scale_grad])
    return (d_kernel, d_chan)

def local_pass(image, cot_image, kernel, chan, w_in, b_in, w_out):
    height, width, channels = image.shape
    rows = height * width
    w_in_low = w_in.astype(jnp.bfloat16)
    w_out_low = w_out.astype(jnp.bfloat16)
    field, scaled, spread, normed = channel_front(image, kernel, chan)
    pre = jnp.dot(normed, w_in_low, preferred_element_type=jnp.float32) + b_in
    hidden = gelu_value(pre).astype(jnp.bfloat16)
    mlp = jnp.dot(hidden, w_out_low, preferred_element_type=jnp.float32) + chan[3]
    output = (image.reshape(rows, channels).astype(jnp.float32) + chan[4] * mlp).astype(jnp.bfloat16)
    cot = cot_image.reshape(rows, channels).astype(jnp.float32)
    bias_grad = lax.optimization_barrier(jnp.sum(cot * chan[4], axis=0))
    scale_grad = lax.optimization_barrier(jnp.sum(cot * mlp, axis=0))
    dmlp = (cot * chan[4]).astype(jnp.bfloat16)
    g_out = jnp.dot(hidden.T, dmlp, preferred_element_type=jnp.float32)
    dhid = jnp.dot(dmlp, w_out_low.T, preferred_element_type=jnp.float32)
    dpre = (dhid * gelu_slope(pre)).astype(jnp.bfloat16)
    g_bin = lax.optimization_barrier(jnp.sum(dpre.astype(jnp.float32), axis=0))
    g_in = jnp.dot(normed.T, dpre, preferred_element_type=jnp.float32)
    dnormed = jnp.dot(dpre, w_in_low.T, preferred_element_type=jnp.float32)
    d_kernel, d_chan = channel_back(field, scaled, spread, dnormed, chan, kernel, bias_grad, scale_grad)
    return (output.reshape(height, width, channels), (d_kernel, d_chan, g_in, g_bin, g_out))

def reference(images, cotangent, dw_kernel, chan_vec, w_in, b_in, w_out, mom_kernel, mom_chan, mom_in, mom_bin, mom_out):
    params = (dw_kernel, chan_vec, w_in, b_in, w_out)
    moments = (mom_kernel, mom_chan, mom_in, mom_bin, mom_out)
    features = None
    for round_index in range(STEPS):

        def replica(packed):
            local_params, image_set, cot_set = packed
            total = None
            outputs = []
            for member in range(GROUPS):
                output, grads = local_pass(image_set[member], cot_set[member], *local_params)
                outputs.append(output)
                total = grads if total is None else tuple((a + b for a, b in zip(total, grads)))
            return (jnp.stack(outputs), total)
        features, summed = lax.map(replica, (params, images[round_index], cotangent[round_index]))
        moments = tuple((MOMENTUM * old + grad for old, grad in zip(moments, summed)))
        stepped = tuple((value - RATE * moment for value, moment in zip(params, moments)))
        distance = 2 ** round_index
        params = tuple((0.5 * (value + jnp.roll(value, distance, axis=0)) for value in stepped))
    return (params[0], params[1], params[2], params[3], params[4], features)
```

```python
import math

import jax
import jax.numpy as jnp
from jax import lax
from jax.experimental import pallas as pl
from jax.experimental.pallas import tpu as pltpu
from jax.sharding import PartitionSpec as P

STEPS = 2


EPS = 1e-06
MOMENTUM = 0.9
RATE = 0.0005
SQRT_HALF = 0.7071067811865476
INV_ROOT_TWO_PI = 0.3989422804014327


def passed_along(block, axis, distance):
    devices = range(lax.axis_size(axis))
    route = [((i - distance) % len(devices), i) for i in devices]
    return lax.ppermute(block, axis, route)


def depthwise(field, kernel):
    channels = kernel.shape[-1]
    reach = math.isqrt(kernel.shape[0])
    margin = reach // 2
    filter_taps = kernel.reshape(reach, reach, 1, channels)
    return lax.conv_general_dilated(
        field,
        filter_taps,
        (1, 1),
        ((margin, margin), (margin, margin)),
        dimension_numbers=("NHWC", "HWIO", "NHWC"),
        feature_group_count=channels,
        precision=lax.Precision.HIGHEST,
    )


def gelu_value(value):
    return 0.5 * value * (1.0 + lax.erf(value * SQRT_HALF))


def gelu_slope(value):
    return (
        0.5 * (1.0 + lax.erf(value * SQRT_HALF))
        + value * jnp.exp(-0.5 * value * value) * INV_ROOT_TWO_PI
    )


def channel_front(image, kernel, chan):
    height, width, channels = image.shape
    field = image.astype(jnp.float32)[None]
    conv = depthwise(field, kernel)[0].reshape(height * width, channels) + chan[0]
    center = conv - jnp.mean(conv, axis=-1, keepdims=True)
    spread = lax.rsqrt(jnp.mean(center * center, axis=-1, keepdims=True) + EPS)
    scaled = center * spread
    normed = (scaled * chan[1] + chan[2]).astype(jnp.bfloat16)
    return (field, scaled, spread, normed)


def channel_back(field, scaled, spread, dnormed, chan, kernel, bias_grad, scale_grad):
    d_gain = jnp.sum(dnormed * scaled, axis=0)
    d_shift = jnp.sum(dnormed, axis=0)
    dscaled = dnormed * chan[1]
    dconv = spread * (
        dscaled
        - jnp.mean(dscaled, axis=-1, keepdims=True)
        - scaled * jnp.mean(dscaled * scaled, axis=-1, keepdims=True)
    )
    d_bias = jnp.sum(dconv, axis=0)
    _, pullback = jax.vjp(lambda taps: depthwise(field, taps), kernel)
    (d_kernel,) = pullback(dconv.reshape(field.shape))
    d_chan = jnp.stack([d_bias, d_gain, d_shift, bias_grad, scale_grad])
    return (d_kernel, d_chan)


def per_device(
    images,
    cotangent,
    dw_kernel,
    chan_vec,
    w_in,
    b_in,
    w_out,
    mom_kernel,
    mom_chan,
    mom_in,
    mom_bin,
    mom_out,
):
    params = (dw_kernel[0], chan_vec[0], w_in[0], b_in[0], w_out[0])
    moments = (mom_kernel[0], mom_chan[0], mom_in[0], mom_bin[0], mom_out[0])
    features = None
    for round_index in range(STEPS):
        kernel, chan, bias_in = (
            lax.all_gather(params[0], "grp", axis=1, tiled=True),
            lax.all_gather(params[1], "grp", axis=1, tiled=True),
            lax.all_gather(params[3], "grp", axis=0, tiled=True),
        )
        in_shard = params[2].astype(jnp.bfloat16)
        out_shard = params[4].astype(jnp.bfloat16)
        image = images[round_index, 0, 0]
        height, width, channels = image.shape
        rows = height * width
        field, scaled, spread, normed = channel_front(image, kernel, chan)
        w_in_full, w_out_full = (
            lax.all_gather(in_shard, "grp", axis=0, tiled=True),
            lax.all_gather(out_shard, "grp", axis=0, tiled=True),
        )
        pre = jnp.dot(normed, w_in_full, preferred_element_type=jnp.float32) + bias_in
        hidden = gelu_value(pre).astype(jnp.bfloat16)
        mlp = jnp.dot(hidden, w_out_full, preferred_element_type=jnp.float32) + chan[3]
        features = (image.reshape(rows, channels).astype(jnp.float32) + chan[4] * mlp).astype(
            jnp.bfloat16
        )
        cot = cotangent[round_index, 0, 0].reshape(rows, channels).astype(jnp.float32)
        bias_grad = jnp.sum(cot * chan[4], axis=0)
        scale_grad = jnp.sum(cot * mlp, axis=0)
        dmlp = (cot * chan[4]).astype(jnp.bfloat16)
        g_out = jnp.dot(hidden.T, dmlp, preferred_element_type=jnp.float32)
        dhid = jnp.dot(dmlp, w_out_full.T, preferred_element_type=jnp.float32)
        dpre = (dhid * gelu_slope(pre)).astype(jnp.bfloat16)
        g_bin = jnp.sum(dpre.astype(jnp.float32), axis=0)
        g_in = jnp.dot(normed.T, dpre, preferred_element_type=jnp.float32)
        dnormed = jnp.dot(dpre, w_in_full.T, preferred_element_type=jnp.float32)
        d_kernel, d_chan = channel_back(
            field, scaled, spread, dnormed, chan, kernel, bias_grad, scale_grad
        )
        sum_kernel, sum_chan, sum_in, sum_bin, sum_out = (
            lax.psum_scatter(
                d_kernel.astype(jnp.bfloat16), "grp", scatter_dimension=1, tiled=True
            ).astype(jnp.float32),
            lax.psum_scatter(
                d_chan.astype(jnp.bfloat16), "grp", scatter_dimension=1, tiled=True
            ).astype(jnp.float32),
            lax.psum_scatter(
                g_in.astype(jnp.bfloat16), "grp", scatter_dimension=0, tiled=True
            ).astype(jnp.float32),
            lax.psum_scatter(
                g_bin.astype(jnp.bfloat16), "grp", scatter_dimension=0, tiled=True
            ).astype(jnp.float32),
            lax.psum_scatter(
                g_out.astype(jnp.bfloat16), "grp", scatter_dimension=0, tiled=True
            ).astype(jnp.float32),
        )
        summed = (sum_kernel, sum_chan, sum_in, sum_bin, sum_out)
        moments = tuple((MOMENTUM * old + grad for old, grad in zip(moments, summed)))
        stepped = tuple((value - RATE * moment for value, moment in zip(params, moments)))
        partner = passed_along(
            (stepped[0], stepped[1], stepped[2], stepped[3], stepped[4]), "peer", 2**round_index
        )
        params = tuple((0.5 * (mine + theirs) for mine, theirs in zip(stepped, partner)))
    return (
        params[0][None],
        params[1][None],
        params[2][None],
        params[3][None],
        params[4][None],
        features.reshape(1, 1, height, width, channels),
    )


BF = jnp.bfloat16
F32 = jnp.float32
CHAN_ROW = 56
SMALL_ROWS = 64
CUT = 256
DEVICE = pl.DeviceIdType.MESH


def dot(a, b, over_a=1, over_b=0):
    return lax.dot_general(
        a, b, (((over_a,), (over_b,)), ((), ())), preferred_element_type=F32
    )


def fused_kernel(
    shape,
    image_ref, cot_ref, kernel_ref, chan_ref, win_ref, bin_ref, wout_ref,
    mkernel_ref, mchan_ref, min_ref, mbin_ref, mout_ref,
    okernel_ref, ochan_ref, oin_ref, obin_ref, oout_ref, ofeat_ref,
    small_mine, small_theirs, small_p, small_m, shifted, scaled_ref, spread_ref,
    normed, cot_theirs, dmlp, hidden, dpre, mlp_ref, mlp_out, mlp_in,
    dnorm_mine, dnorm_out, dnorm_in, dconv_ref, tap_grad, small_grad, grad_out, grad_in,
    gossip_small_out, gossip_small_in, bias_p, bias_m, bias_out, bias_in, bias_grad_ref,
    w_stage, m_stage, m_theirs, w_in_low, w_in_full, m_in_full, w_out_low, w_out_full, m_out_full,
    q_out_send, q_out_recv, q_in_send, q_in_recv, last_send, last_recv,
    send_sem, recv_sem,
):
    height, width, channels, hid = shape
    rows = height * width
    half = channels // 2
    reach = math.isqrt(kernel_ref.shape[0])
    margin = reach // 2
    taps = reach * reach
    peers = lax.axis_size("peer")
    me = lax.axis_index("peer")
    grp = lax.axis_index("grp")
    other = 1 - grp
    pair = (me, other)

    barrier = pltpu.get_barrier_semaphore()
    pl.semaphore_signal(barrier, inc=1, device_id=pair, device_id_type=DEVICE)
    for step in range(STEPS):
        source = (lax.rem(me + peers - 2**step, peers), grp)
        pl.semaphore_signal(barrier, inc=1, device_id=source, device_id_type=DEVICE)

    started = []

    def push(src, dst, device):
        at = len(started)
        copy = pltpu.make_async_remote_copy(
            src_ref=src, dst_ref=dst, send_sem=send_sem.at[at], recv_sem=recv_sem.at[at],
            device_id=device, device_id_type=DEVICE,
        )
        copy.start()
        started.append(copy)
        return copy

    my_rows = pl.ds(pl.multiple_of(grp * half, 16), half)
    their_rows = pl.ds(pl.multiple_of(other * half, 16), half)
    my_cols = pl.ds(pl.multiple_of(grp * hid, 128), hid)
    their_cols = pl.ds(pl.multiple_of(other * hid, 128), hid)

    small_mine[...] = jnp.zeros_like(small_mine)
    small_mine[0, 0:taps, :] = kernel_ref[...]
    small_mine[0, CHAN_ROW : CHAN_ROW + 5, :] = chan_ref[...]
    small_mine[1, 0:taps, :] = mkernel_ref[...]
    small_mine[1, CHAN_ROW : CHAN_ROW + 5, :] = mchan_ref[...]
    w_stage[...] = win_ref[:, their_cols].astype(BF)
    pl.semaphore_wait(barrier, 1 + STEPS)
    small_copy = push(small_mine, small_theirs, pair)
    w_copy = push(w_stage, w_in_low.at[0, my_rows, :], pair)

    w_in_low[0, my_rows, :] = win_ref[:, my_cols].astype(BF)
    w_in_full[my_rows, :] = win_ref[:, my_cols]
    m_in_full[my_rows, :] = min_ref[:, my_cols]
    m_stage[...] = min_ref[:, their_cols].astype(BF)
    w_out_low[0] = wout_ref[...].astype(BF)
    bias_p[...] = bin_ref[...]
    bias_m[...] = mbin_ref[...]

    def shift_rows(step):
        shifted[:, 0:margin] = jnp.zeros((reach, margin, width, channels), F32)
        shifted[:, margin + height :] = jnp.zeros((reach, margin, width, channels), F32)
        column = lax.broadcasted_iota(jnp.int32, (width, channels), 0)

        def body(i, _):
            x = image_ref[step, pl.ds(pl.multiple_of(i * width, width), width), :].astype(F32)
            for j in range(reach):
                off = j - margin
                moved = x if off == 0 else pltpu.roll(x, (-off) % width, 0)
                inside = (column + off >= 0) & (column + off < width)
                shifted[j, i + margin] = jnp.where(inside, moved, 0.0)
            return 0

        lax.fori_loop(0, height, body, 0)

    def front(step):
        bias, gain, shift = (small_p[CHAN_ROW + k : CHAN_ROW + k + 1, :] for k in range(3))

        def body(i, _):
            conv = jnp.zeros((width, channels), F32)
            for t in range(taps):
                conv = conv + shifted[t % reach, i + t // reach] * small_p[t : t + 1, :]
            conv = conv + bias
            center = conv - jnp.mean(conv, axis=-1, keepdims=True)
            spread = lax.rsqrt(jnp.mean(center * center, axis=-1, keepdims=True) + EPS)
            scaled = center * spread
            at = pl.ds(pl.multiple_of(i * width, width), width)
            scaled_ref[at, :] = scaled
            spread_ref[at, :] = spread
            normed[step, at, :] = (scaled * gain + shift).astype(BF)
            return 0

        lax.fori_loop(0, height, body, 0)

    def through(step, place):
        at = slice(place * rows, (place + 1) * rows)
        scale = small_p[CHAN_ROW + 4 : CHAN_ROW + 5, :]
        cot = (cot_ref[step] if place == 0 else cot_theirs[step]).astype(F32)
        dmlp[at, :] = (cot * scale).astype(BF)

        def body(c, _):
            cut = pl.ds(pl.multiple_of(c * CUT, CUT), CUT)
            pre = dot(normed[step, at, :], w_in_low[step, :, cut]) + bias_p[0:1, cut]
            bell = 0.5 * (1.0 + lax.erf(pre * SQRT_HALF))
            hidden[at, cut] = (pre * bell).astype(BF)
            slope = bell + pre * jnp.exp(-0.5 * pre * pre) * INV_ROOT_TWO_PI
            dhid = dot(dmlp[at, :], w_out_low[step, cut, :], 1, 1)
            dpre[at, cut] = (dhid * slope).astype(BF)
            return 0

        lax.fori_loop(0, hid // CUT, body, 0)
        dnorm = dot(dpre[at, :], w_in_low[step], 1, 1)
        return cot, dnorm, at

    def take_gossip(step, low):
        for copy in gossip["out"]:
            copy.wait_recv()
        value = 0.5 * (w_out_full[...] + q_out_recv[step].astype(F32))
        w_out_full[...] = value
        low[...] = value.astype(low.dtype)

    shift_rows(0)
    small_copy.wait_recv()
    for k, full in enumerate((small_p, small_m)):
        mine, theirs = small_mine[k], small_theirs[k]
        first = jnp.where(grp == 0, mine, theirs)
        second = jnp.where(grp == 0, theirs, mine)
        full[...] = jnp.concatenate([first, second], axis=1)

    for step in range(STEPS):
        front(step)
        normed_copy = push(normed.at[step, 0:rows], normed.at[step, rows : 2 * rows], pair)
        if step == 0:
            cot_copy = push(cot_ref.at[0], cot_theirs.at[0], pair)
            w_copy.wait_recv()
        else:
            take_gossip(0, w_out_low.at[1])
            for copy in gossip["in"]:
                copy.wait_recv()
            value = 0.5 * (w_in_full[...] + q_in_recv[0].astype(F32))
            w_in_full[...] = value
            w_in_low[1] = value.astype(BF)
            gossip["bias"].wait_recv()
            bias_p[...] = 0.5 * (bias_p[...] + bias_in[0, 0:1, :])

        cot, dnorm, at = through(step, 0)
        dnorm_mine[...] = dnorm
        mlp = dot(hidden[at, :], w_out_low[step])
        mlp_ref[...] = mlp
        scale_grad = jnp.sum(cot * mlp, axis=0, keepdims=True)
        cot_sum = jnp.sum(cot, axis=0, keepdims=True)
        scale_grad = scale_grad + cot_sum * small_p[CHAN_ROW + 3 : CHAN_ROW + 4, :]
        bias_grad = jnp.sum(cot * small_p[CHAN_ROW + 4 : CHAN_ROW + 5, :], axis=0, keepdims=True)

        normed_copy.wait_recv()
        cot_copy.wait_recv()
        cot, dnorm, at = through(step, 1)
        dnorm_out[step] = dnorm.astype(BF)
        dnorm_copy = push(dnorm_out.at[step], dnorm_in.at[step], pair)
        mlp = dot(hidden[at, :], w_out_low[step])
        scale_grad = scale_grad + jnp.sum(cot * mlp, axis=0, keepdims=True)
        if step == STEPS - 1:
            mlp_out[...] = mlp.astype(BF)
            mlp_copy = push(mlp_out, mlp_in, pair)
        else:
            m_copy = push(m_stage, m_theirs, pair)

        onward = (lax.rem(me + 2**step, peers), grp)
        gossip = {"out": [], "in": []}
        if step == 0:
            m_out_full[...] = mout_ref[...]
            w_out_full[...] = wout_ref[...]
        for c in range(hid // CUT):
            cut = slice(c * CUT, (c + 1) * CUT)
            grad = dot(hidden[:, cut], dmlp[...], 0, 0)
            moment = MOMENTUM * m_out_full[cut, :] + grad
            m_out_full[cut, :] = moment
            stepped = w_out_full[cut, :] - RATE * moment
            w_out_full[cut, :] = stepped
            q_out_send[step, cut, :] = stepped.astype(BF)
            gossip["out"].append(push(q_out_send.at[step, cut], q_out_recv.at[step, cut], onward))
        bias_moment = MOMENTUM * bias_m[...] + jnp.sum(dpre[...].astype(F32), axis=0, keepdims=True)
        bias_m[...] = bias_moment
        bias_p[...] = bias_p[...] - RATE * bias_moment
        bias_out[step] = jnp.broadcast_to(bias_p[...], bias_out.shape[1:])
        gossip["bias"] = push(bias_out.at[step], bias_in.at[step], onward)

        if step == 0:
            m_copy.wait_recv()
            m_in_full[their_rows, :] = m_theirs[...].astype(F32)
            w_in_full[their_rows, :] = w_in_low[0, their_rows, :].astype(F32)
        pieces = channels // 128
        for c in range(pieces):
            cut = slice(c * 128, (c + 1) * 128)
            grad = dot(normed[step, :, cut], dpre[...], 0, 0)
            moment = MOMENTUM * m_in_full[cut, :] + grad
            m_in_full[cut, :] = moment
            stepped = w_in_full[cut, :] - RATE * moment
            w_in_full[cut, :] = stepped
            q_in_send[step, cut, :] = stepped.astype(BF)
            gossip["in"].append(push(q_in_send.at[step, cut], q_in_recv.at[step, cut], onward))

        dnorm_copy.wait_recv()
        gain = small_p[CHAN_ROW + 1 : CHAN_ROW + 2, :]
        zero = jnp.zeros((1, channels), F32)

        def back(i, sums):
            at = pl.ds(pl.multiple_of(i * width, width), width)
            dn = dnorm_mine[at, :] + dnorm_in[step, at, :].astype(F32)
            scaled = scaled_ref[at, :]
            ds = dn * gain
            dconv = spread_ref[at, :] * (
                ds
                - jnp.mean(ds, axis=-1, keepdims=True)
                - scaled * jnp.mean(ds * scaled, axis=-1, keepdims=True)
            )
            dconv_ref[i] = dconv
            return (
                sums[0] + jnp.sum(dconv, axis=0, keepdims=True),
                sums[1] + jnp.sum(dn * scaled, axis=0, keepdims=True),
                sums[2] + jnp.sum(dn, axis=0, keepdims=True),
            )

        sums = lax.fori_loop(0, height, back, (zero, zero, zero))

        def tap_column(j, _):
            for b in range(channels // 128):
                lanes = slice(b * 128, (b + 1) * 128)
                got = []
                for d in range(reach):
                    total = jnp.zeros((width, 128), F32)
                    for i in range(height):
                        total = total + shifted[j, i + d, :, lanes] * dconv_ref[i, :, lanes]
                    got.append(jnp.sum(total, axis=0, keepdims=True))
                for d in range(reach):
                    tap_grad[j, d : d + 1, lanes] = got[d]
            return 0

        lax.fori_loop(0, reach, tap_column, 0)
        small_grad[...] = jnp.zeros_like(small_grad)
        for t in range(taps):
            small_grad[t : t + 1, :] = tap_grad[t % reach, t // reach : t // reach + 1, :]
        for k, value in enumerate((*sums, bias_grad, scale_grad)):
            small_grad[CHAN_ROW + k : CHAN_ROW + k + 1, :] = value
        grad_out[step] = small_grad[...].astype(BF)
        grad_copy = push(grad_out.at[step], grad_in.at[step], pair)
        if step + 1 < STEPS:
            shift_rows(step + 1)
        else:
            mlp_copy.wait_recv()
            mlp = mlp_ref[...] + mlp_in[...].astype(F32) + small_p[CHAN_ROW + 3 : CHAN_ROW + 4, :]
            ofeat_ref[...] = (
                image_ref[step].astype(F32) + small_p[CHAN_ROW + 4 : CHAN_ROW + 5, :] * mlp
            ).astype(BF)
        grad_copy.wait_recv()
        moment = MOMENTUM * small_m[...] + (grad_out[step].astype(F32) + grad_in[step].astype(F32))
        small_m[...] = moment
        stepped = small_p[...] - RATE * moment
        gossip_small_out[step] = stepped.astype(BF)
        small_gossip = push(gossip_small_out.at[step], gossip_small_in.at[step], onward)
        if step + 1 < STEPS:
            cot_copy = push(cot_ref.at[step + 1], cot_theirs.at[step + 1], pair)
        small_gossip.wait_recv()
        small_p[...] = 0.5 * (stepped + gossip_small_in[step].astype(F32))

    def mine_of(value):
        return jnp.where(grp == 0, value[:, 0:half], value[:, half:])

    okernel_ref[...] = mine_of(small_p[0:taps, :])
    ochan_ref[...] = mine_of(small_p[CHAN_ROW : CHAN_ROW + 5, :])
    last = STEPS - 1
    take_gossip(last, oout_ref)
    gossip["bias"].wait_recv()
    obin_ref[...] = 0.5 * (bias_p[...] + bias_in[last, 0:1, :])
    for copy in gossip["in"]:
        copy.wait_recv()
    last_send[...] = (
        0.5 * (w_in_full[their_rows, :] + q_in_recv[last, their_rows, :].astype(F32))
    ).astype(BF)
    last_copy = push(last_send, last_recv, pair)
    oin_ref[:, my_cols] = 0.5 * (w_in_full[my_rows, :] + q_in_recv[last, my_rows, :].astype(F32))
    last_copy.wait_recv()
    oin_ref[:, their_cols] = last_recv[...].astype(F32)
    for copy in started:
        copy.wait_send()


def fused_device(
    images, cotangent, dw_kernel, chan_vec, w_in, b_in, w_out,
    mom_kernel, mom_chan, mom_in, mom_bin, mom_out,
):
    steps, _, _, height, width, channels = images.shape
    rows = height * width
    taps, half = dw_kernel.shape[1:]
    reach = math.isqrt(taps)
    margin = reach // 2
    hid = b_in.shape[1]
    V = pltpu.VMEM
    scratch = [
        V((2, SMALL_ROWS, half), F32), V((2, SMALL_ROWS, half), F32),
        V((SMALL_ROWS, channels), F32), V((SMALL_ROWS, channels), F32),
        V((reach, height + 2 * margin, width, channels), F32),
        V((rows, channels), F32), V((rows, 1), F32),
        V((steps, 2 * rows, channels), BF), V((steps, rows, channels), BF),
        V((2 * rows, channels), BF), V((2 * rows, hid), BF), V((2 * rows, hid), BF),
        V((rows, channels), F32), V((rows, channels), BF), V((rows, channels), BF),
        V((rows, channels), F32), V((steps, rows, channels), BF), V((steps, rows, channels), BF),
        V((height, width, channels), F32), V((reach, 8, channels), F32),
        V((SMALL_ROWS, channels), F32),
        V((steps, SMALL_ROWS, channels), BF), V((steps, SMALL_ROWS, channels), BF),
        V((steps, SMALL_ROWS, channels), BF), V((steps, SMALL_ROWS, channels), BF),
        V((1, hid), F32), V((1, hid), F32),
        V((steps, 8, hid), F32), V((steps, 8, hid), F32), V((1, hid), F32),
        V((half, hid), BF), V((half, hid), BF), V((half, hid), BF),
        V((steps, channels, hid), BF), V((channels, hid), F32), V((channels, hid), F32),
        V((steps, hid, channels), BF), V((hid, channels), F32), V((hid, channels), F32),
        V((steps, hid, channels), BF), V((steps, hid, channels), BF),
        V((steps, channels, hid), BF), V((steps, channels, hid), BF),
        V((half, hid), BF), V((half, hid), BF),
        pltpu.SemaphoreType.DMA((40,)), pltpu.SemaphoreType.DMA((40,)),
    ]
    shapes = [
        jax.ShapeDtypeStruct((taps, half), F32),
        jax.ShapeDtypeStruct(chan_vec.shape[1:], F32),
        jax.ShapeDtypeStruct(w_in.shape[1:], F32),
        jax.ShapeDtypeStruct((1, hid), F32),
        jax.ShapeDtypeStruct(w_out.shape[1:], F32),
        jax.ShapeDtypeStruct((rows, channels), BF),
    ]
    whole = pl.BlockSpec(memory_space=pltpu.VMEM)
    out = pl.pallas_call(
        lambda *refs: fused_kernel((height, width, channels, hid), *refs),
        out_shape=shapes,
        in_specs=[whole] * 12,
        out_specs=[whole] * 6,
        scratch_shapes=scratch,
        compiler_params=pltpu.CompilerParams(
            collective_id=0, has_side_effects=True, vmem_limit_bytes=56 * 2**20
        ),
    )(
        images.reshape(steps, rows, channels), cotangent.reshape(steps, rows, channels),
        dw_kernel[0], chan_vec[0], w_in[0], b_in, w_out[0],
        mom_kernel[0], mom_chan[0], mom_in[0], mom_bin, mom_out[0],
    )
    return (
        out[0][None], out[1][None], out[2][None], out[3], out[4][None],
        out[5].reshape(1, 1, height, width, channels),
    )


def solution(mesh):
    fused = mesh.shape["grp"] == 2 and mesh.shape["peer"] > 4
    return jax.shard_map(
        fused_device if fused else per_device,
        mesh=mesh,
        in_specs=(
            P(None, "peer", "grp", None, None, None),
            P(None, "peer", "grp", None, None, None),
            P("peer", None, "grp"),
            P("peer", None, "grp"),
            P("peer", "grp", None),
            P("peer", "grp"),
            P("peer", "grp", None),
            P("peer", None, "grp"),
            P("peer", None, "grp"),
            P("peer", "grp", None),
            P("peer", "grp"),
            P("peer", "grp", None),
        ),
        out_specs=(
            P("peer", None, "grp"),
            P("peer", None, "grp"),
            P("peer", "grp", None),
            P("peer", "grp"),
            P("peer", "grp", None),
            P("peer", "grp", None, None, None),
        ),
        check_vma=False,
    )
```

```python
import math

import jax
import jax.numpy as jnp
from jax import lax
from jax.experimental import pallas as pl
from jax.experimental.pallas import tpu as pltpu
from jax.sharding import PartitionSpec as P

STEPS = 2


EPS = 1e-06
MOMENTUM = 0.9
RATE = 0.0005
SQRT_HALF = 0.7071067811865476
INV_ROOT_TWO_PI = 0.3989422804014327


def passed_along(block, axis, distance):
    devices = range(lax.axis_size(axis))
    route = [((i - distance) % len(devices), i) for i in devices]
    return lax.ppermute(block, axis, route)


def depthwise(field, kernel):
    channels = kernel.shape[-1]
    reach = math.isqrt(kernel.shape[0])
    margin = reach // 2
    filter_taps = kernel.reshape(reach, reach, 1, channels)
    return lax.conv_general_dilated(
        field,
        filter_taps,
        (1, 1),
        ((margin, margin), (margin, margin)),
        dimension_numbers=("NHWC", "HWIO", "NHWC"),
        feature_group_count=channels,
        precision=lax.Precision.HIGHEST,
    )


def gelu_value(value):
    return 0.5 * value * (1.0 + lax.erf(value * SQRT_HALF))


def gelu_slope(value):
    return (
        0.5 * (1.0 + lax.erf(value * SQRT_HALF))
        + value * jnp.exp(-0.5 * value * value) * INV_ROOT_TWO_PI
    )


def channel_front(image, kernel, chan):
    height, width, channels = image.shape
    field = image.astype(jnp.float32)[None]
    conv = depthwise(field, kernel)[0].reshape(height * width, channels) + chan[0]
    center = conv - jnp.mean(conv, axis=-1, keepdims=True)
    spread = lax.rsqrt(jnp.mean(center * center, axis=-1, keepdims=True) + EPS)
    scaled = center * spread
    normed = (scaled * chan[1] + chan[2]).astype(jnp.bfloat16)
    return (field, scaled, spread, normed)


def channel_back(field, scaled, spread, dnormed, chan, kernel, bias_grad, scale_grad):
    d_gain = jnp.sum(dnormed * scaled, axis=0)
    d_shift = jnp.sum(dnormed, axis=0)
    dscaled = dnormed * chan[1]
    dconv = spread * (
        dscaled
        - jnp.mean(dscaled, axis=-1, keepdims=True)
        - scaled * jnp.mean(dscaled * scaled, axis=-1, keepdims=True)
    )
    d_bias = jnp.sum(dconv, axis=0)
    _, pullback = jax.vjp(lambda taps: depthwise(field, taps), kernel)
    (d_kernel,) = pullback(dconv.reshape(field.shape))
    d_chan = jnp.stack([d_bias, d_gain, d_shift, bias_grad, scale_grad])
    return (d_kernel, d_chan)


def per_device(
    images,
    cotangent,
    dw_kernel,
    chan_vec,
    w_in,
    b_in,
    w_out,
    mom_kernel,
    mom_chan,
    mom_in,
    mom_bin,
    mom_out,
):
    params = (dw_kernel[0], chan_vec[0], w_in[0], b_in[0], w_out[0])
    moments = (mom_kernel[0], mom_chan[0], mom_in[0], mom_bin[0], mom_out[0])
    features = None
    for round_index in range(STEPS):
        kernel, chan, bias_in = (
            lax.all_gather(params[0], "grp", axis=1, tiled=True),
            lax.all_gather(params[1], "grp", axis=1, tiled=True),
            lax.all_gather(params[3], "grp", axis=0, tiled=True),
        )
        in_shard = params[2].astype(jnp.bfloat16)
        out_shard = params[4].astype(jnp.bfloat16)
        image = images[round_index, 0, 0]
        height, width, channels = image.shape
        rows = height * width
        field, scaled, spread, normed = channel_front(image, kernel, chan)
        w_in_full, w_out_full = (
            lax.all_gather(in_shard, "grp", axis=0, tiled=True),
            lax.all_gather(out_shard, "grp", axis=0, tiled=True),
        )
        pre = jnp.dot(normed, w_in_full, preferred_element_type=jnp.float32) + bias_in
        hidden = gelu_value(pre).astype(jnp.bfloat16)
        mlp = jnp.dot(hidden, w_out_full, preferred_element_type=jnp.float32) + chan[3]
        features = (image.reshape(rows, channels).astype(jnp.float32) + chan[4] * mlp).astype(
            jnp.bfloat16
        )
        cot = cotangent[round_index, 0, 0].reshape(rows, channels).astype(jnp.float32)
        bias_grad = jnp.sum(cot * chan[4], axis=0)
        scale_grad = jnp.sum(cot * mlp, axis=0)
        dmlp = (cot * chan[4]).astype(jnp.bfloat16)
        g_out = jnp.dot(hidden.T, dmlp, preferred_element_type=jnp.float32)
        dhid = jnp.dot(dmlp, w_out_full.T, preferred_element_type=jnp.float32)
        dpre = (dhid * gelu_slope(pre)).astype(jnp.bfloat16)
        g_bin = jnp.sum(dpre.astype(jnp.float32), axis=0)
        g_in = jnp.dot(normed.T, dpre, preferred_element_type=jnp.float32)
        dnormed = jnp.dot(dpre, w_in_full.T, preferred_element_type=jnp.float32)
        d_kernel, d_chan = channel_back(
            field, scaled, spread, dnormed, chan, kernel, bias_grad, scale_grad
        )
        sum_kernel, sum_chan, sum_in, sum_bin, sum_out = (
            lax.psum_scatter(
                d_kernel.astype(jnp.bfloat16), "grp", scatter_dimension=1, tiled=True
            ).astype(jnp.float32),
            lax.psum_scatter(
                d_chan.astype(jnp.bfloat16), "grp", scatter_dimension=1, tiled=True
            ).astype(jnp.float32),
            lax.psum_scatter(
                g_in.astype(jnp.bfloat16), "grp", scatter_dimension=0, tiled=True
            ).astype(jnp.float32),
            lax.psum_scatter(
                g_bin.astype(jnp.bfloat16), "grp", scatter_dimension=0, tiled=True
            ).astype(jnp.float32),
            lax.psum_scatter(
                g_out.astype(jnp.bfloat16), "grp", scatter_dimension=0, tiled=True
            ).astype(jnp.float32),
        )
        summed = (sum_kernel, sum_chan, sum_in, sum_bin, sum_out)
        moments = tuple((MOMENTUM * old + grad for old, grad in zip(moments, summed)))
        stepped = tuple((value - RATE * moment for value, moment in zip(params, moments)))
        partner = passed_along(
            (stepped[0], stepped[1], stepped[2], stepped[3], stepped[4]), "peer", 2**round_index
        )
        params = tuple((0.5 * (mine + theirs) for mine, theirs in zip(stepped, partner)))
    return (
        params[0][None],
        params[1][None],
        params[2][None],
        params[3][None],
        params[4][None],
        features.reshape(1, 1, height, width, channels),
    )


BF = jnp.bfloat16
F32 = jnp.float32
CHAN_ROW = 56
SMALL_ROWS = 64
CUT = 256
DEVICE = pl.DeviceIdType.MESH


def dot(a, b, over_a=1, over_b=0):
    return lax.dot_general(
        a, b, (((over_a,), (over_b,)), ((), ())), preferred_element_type=F32
    )


def fused_kernel(
    shape,
    image_ref, cot_ref, kernel_ref, chan_ref, win_ref, bin_ref, wout_ref,
    mkernel_ref, mchan_ref, min_ref, mbin_ref, mout_ref,
    okernel_ref, ochan_ref, oin_ref, obin_ref, oout_ref, ofeat_ref,
    small_mine, small_theirs, small_p, small_m, shifted, scaled_ref, spread_ref,
    normed, cot_theirs, dmlp, hidden, dpre, mlp_ref, mlp_out, mlp_in,
    dnorm_mine, dnorm_out, dnorm_in, dconv_ref, tap_grad, small_grad, grad_out, grad_in,
    gossip_small_out, gossip_small_in, bias_p, bias_m, bias_out, bias_in, bias_grad_ref,
    w_stage, m_stage, m_theirs, w_in_low, w_in_full, m_in_full, w_out_low, w_out_full, m_out_full,
    q_out_send, q_out_recv, q_in_send, q_in_recv, last_send, last_recv,
    normed_t, in_grad, m_in_rows, send_sem, recv_sem, load_sem,
):
    height, width, channels, hid = shape
    rows = height * width
    half = channels // 2
    reach = math.isqrt(kernel_ref.shape[0])
    margin = reach // 2
    taps = reach * reach
    peers = lax.axis_size("peer")
    me = lax.axis_index("peer")
    grp = lax.axis_index("grp")
    other = 1 - grp
    pair = (me, other)

    barrier = pltpu.get_barrier_semaphore()
    pl.semaphore_signal(barrier, inc=1, device_id=pair, device_id_type=DEVICE)
    for step in range(STEPS):
        source = (lax.rem(me + peers - 2**step, peers), grp)
        pl.semaphore_signal(barrier, inc=1, device_id=source, device_id_type=DEVICE)

    loads = [
        pltpu.make_async_copy(src, dst, load_sem.at[k])
        for k, (src, dst) in enumerate(
            ((wout_ref, w_out_full), (mout_ref, m_out_full), (min_ref, m_in_rows))
        )
    ]
    for load in loads:
        load.start()
    started = []

    def push(src, dst, device):
        at = len(started)
        copy = pltpu.make_async_remote_copy(
            src_ref=src, dst_ref=dst, send_sem=send_sem.at[at], recv_sem=recv_sem.at[at],
            device_id=device, device_id_type=DEVICE,
        )
        copy.start()
        started.append(copy)
        return copy

    my_rows = pl.ds(pl.multiple_of(grp * half, 16), half)
    their_rows = pl.ds(pl.multiple_of(other * half, 16), half)
    my_cols = pl.ds(pl.multiple_of(grp * hid, 128), hid)
    their_cols = pl.ds(pl.multiple_of(other * hid, 128), hid)

    small_mine[...] = jnp.zeros_like(small_mine)
    small_mine[0, 0:taps, :] = kernel_ref[:, 0, :]
    small_mine[0, CHAN_ROW : CHAN_ROW + 5, :] = chan_ref[:, 0, :]
    w_stage[...] = win_ref[:, their_cols].astype(BF)
    pl.semaphore_wait(barrier, 1 + STEPS)
    small_copy = push(small_mine.at[0], small_theirs.at[0], pair)
    w_copy = push(w_stage, w_in_low.at[0, my_rows, :], pair)
    small_mine[1, 0:taps, :] = mkernel_ref[:, 0, :]
    small_mine[1, CHAN_ROW : CHAN_ROW + 5, :] = mchan_ref[:, 0, :]

    w_in_low[0, my_rows, :] = win_ref[:, my_cols].astype(BF)
    w_in_full[my_rows, :] = win_ref[:, my_cols]
    bias_p[...] = bin_ref[...]
    bias_m[...] = mbin_ref[...]

    def shift_rows(step):
        shifted[:, 0:margin] = jnp.zeros((reach, margin, width, channels), F32)
        shifted[:, margin + height :] = jnp.zeros((reach, margin, width, channels), F32)
        column = lax.broadcasted_iota(jnp.int32, (width, channels), 0)

        def body(i, _):
            x = image_ref[step, pl.ds(pl.multiple_of(i * width, width), width), :].astype(F32)
            for j in range(reach):
                off = j - margin
                moved = x if off == 0 else pltpu.roll(x, (-off) % width, 0)
                inside = (column + off >= 0) & (column + off < width)
                shifted[j, i + margin] = jnp.where(inside, moved, 0.0)
            return 0

        lax.fori_loop(0, height, body, 0)

    def front(step):
        bias, gain, shift = (small_p[CHAN_ROW + k : CHAN_ROW + k + 1, :] for k in range(3))

        def body(i, _):
            conv = jnp.zeros((width, channels), F32)
            for t in range(taps):
                conv = conv + shifted[t % reach, i + t // reach] * small_p[t : t + 1, :]
            conv = conv + bias
            center = conv - jnp.mean(conv, axis=-1, keepdims=True)
            spread = lax.rsqrt(jnp.mean(center * center, axis=-1, keepdims=True) + EPS)
            scaled = center * spread
            at = pl.ds(pl.multiple_of(i * width, width), width)
            scaled_ref[at, :] = scaled
            spread_ref[at, :] = spread
            normed[step, at, :] = (scaled * gain + shift).astype(BF)
            return 0

        copies = []
        for h in range(2):
            lax.fori_loop(h * height // 2, (h + 1) * height // 2, body, 0)
            at = slice(h * rows // 2, (h + 1) * rows // 2)
            theirs = slice(rows + at.start, rows + at.stop)
            copies.append(push(normed.at[step, at], normed.at[step, theirs], pair))
        return copies

    def through(step, place, after=None):
        at = slice(place * rows, (place + 1) * rows)
        scale = small_p[CHAN_ROW + 4 : CHAN_ROW + 5, :]
        cot = (cot_ref[step] if place == 0 else cot_theirs[step]).astype(F32)
        dmlp[at, :] = (cot * scale).astype(BF)

        def body(c, _):
            cut = pl.ds(pl.multiple_of(c * CUT, CUT), CUT)
            pre = dot(normed[step, at, :], w_in_low[step, :, cut]) + bias_p[0:1, cut]
            bell = 0.5 * (1.0 + lax.erf(pre * SQRT_HALF))
            hidden[at, cut] = (pre * bell).astype(BF)
            slope = bell + pre * jnp.exp(-0.5 * pre * pre) * INV_ROOT_TWO_PI
            dhid = dot(dmlp[at, :], w_out_low[step, cut, :], 1, 1)
            dpre[at, cut] = (dhid * slope).astype(BF)
            return 0

        if after is None:
            lax.fori_loop(0, hid // CUT, body, 0)
        else:
            for c in range(hid // CUT):
                body(c, 0)
                after(c)
        return cot, at

    def in_update(step, c, grad):
        cut = slice(c * CUT, (c + 1) * CUT)
        moment = MOMENTUM * m_in_full[:, cut] + grad
        m_in_full[:, cut] = moment
        stepped = w_in_full[:, cut] - RATE * moment
        w_in_full[:, cut] = stepped
        q_in_send[step, c] = stepped.astype(BF)
        gossip["in"].append(push(q_in_send.at[step, c], q_in_recv.at[step, c], onward))

    def in_gradient(step, c):
        return dot(normed_t[...], dpre[:, c * CUT : (c + 1) * CUT])

    def out_updates(step):
        for c in range(hid // CUT):
            cut = slice(c * CUT, (c + 1) * CUT)
            grad = dot(hidden[:, cut], dmlp[...], 0, 0)
            moment = MOMENTUM * m_out_full[cut, :] + grad
            m_out_full[cut, :] = moment
            stepped = w_out_full[cut, :] - RATE * moment
            w_out_full[cut, :] = stepped
            q_out_send[step, cut, :] = stepped.astype(BF)
            gossip["out"].append(push(q_out_send.at[step, cut], q_out_recv.at[step, cut], onward))

    def bias_update(step):
        bias_moment = MOMENTUM * bias_m[...] + jnp.sum(dpre[...].astype(F32), axis=0, keepdims=True)
        bias_m[...] = bias_moment
        bias_p[...] = bias_p[...] - RATE * bias_moment
        bias_out[step] = jnp.broadcast_to(bias_p[...], bias_out.shape[1:])
        gossip["bias"] = push(bias_out.at[step], bias_in.at[step], onward)

    shift_rows(0)

    def join(k, full):
        mine, theirs = small_mine[k], small_theirs[k]
        first = jnp.where(grp == 0, mine, theirs)
        second = jnp.where(grp == 0, theirs, mine)
        full[...] = jnp.concatenate([first, second], axis=1)

    small_copy.wait_recv()
    join(0, small_p)

    for step in range(STEPS):
        normed_copies = front(step)
        if step == 0:
            cot_copy = push(cot_ref.at[0], cot_theirs.at[0], pair)
            loads[0].wait()
            w_out_low[0] = w_out_full[...].astype(BF)
            w_copy.wait_recv()
        else:
            for c, copy in enumerate(gossip["out"]):
                cut = slice(c * CUT, (c + 1) * CUT)
                copy.wait_recv()
                value = 0.5 * (w_out_full[cut, :] + q_out_recv[0, cut, :].astype(F32))
                w_out_full[cut, :] = value
                w_out_low[1, cut, :] = value.astype(BF)
            for c, copy in enumerate(gossip["in"]):
                cut = slice(c * CUT, (c + 1) * CUT)
                copy.wait_recv()
                value = 0.5 * (w_in_full[:, cut] + q_in_recv[0, c].astype(F32))
                w_in_full[:, cut] = value
                w_in_low[1, :, cut] = value.astype(BF)
            gossip["bias"].wait_recv()
            bias_p[...] = 0.5 * (bias_p[...] + bias_in[0, 0:1, :])
        onward = (lax.rem(me + 2**step, peers), grp)
        gossip = {"out": [], "in": []}

        cot, at = through(step, 0)
        dnorm_mine[...] = dot(dpre[at, :], w_in_low[step], 1, 1)
        mlp = dot(hidden[at, :], w_out_low[step])
        mlp_ref[...] = mlp
        normed_t[:, at] = normed[step, at, :].T
        scale_grad = jnp.sum(cot * mlp, axis=0, keepdims=True)
        cot_sum = jnp.sum(cot, axis=0, keepdims=True)
        scale_grad = scale_grad + cot_sum * small_p[CHAN_ROW + 3 : CHAN_ROW + 4, :]
        bias_grad = jnp.sum(cot * small_p[CHAN_ROW + 4 : CHAN_ROW + 5, :], axis=0, keepdims=True)
        if step == 0:
            loads[1].wait()
            loads[2].wait()
            m_in_full[my_rows, :] = m_in_rows[:, my_cols]
            m_stage[...] = m_in_rows[:, their_cols].astype(BF)

        for copy in normed_copies:
            copy.wait_recv()
        normed_t[:, rows : 2 * rows] = normed[step, rows : 2 * rows, :].T
        cot_copy.wait_recv()
        final = step == STEPS - 1
        after = (lambda c: in_update(step, c, in_gradient(step, c))) if final else None
        cot, at = through(step, 1, after)
        dnorm_out[step] = dot(dpre[at, :], w_in_low[step], 1, 1).astype(BF)
        dnorm_copy = push(dnorm_out.at[step], dnorm_in.at[step], pair)
        out_updates(step)
        mlp = dot(hidden[at, :], w_out_low[step])
        scale_grad = scale_grad + jnp.sum(cot * mlp, axis=0, keepdims=True)
        bias_update(step)
        if final:
            mlp_out[...] = mlp.astype(BF)
        else:
            for c in range(hid // CUT):
                in_grad[:, c * CUT : (c + 1) * CUT] = in_gradient(step, c)

        dnorm_copy.wait_recv()
        if final:
            mlp_copy = push(mlp_out, mlp_in, pair)
        else:
            small_m_copy = push(small_mine.at[1], small_theirs.at[1], pair)
            m_copy = push(m_stage, m_theirs, pair)
        gain = small_p[CHAN_ROW + 1 : CHAN_ROW + 2, :]
        zero = jnp.zeros((1, channels), F32)

        def back(i, sums):
            at = pl.ds(pl.multiple_of(i * width, width), width)
            dn = dnorm_mine[at, :] + dnorm_in[step, at, :].astype(F32)
            scaled = scaled_ref[at, :]
            ds = dn * gain
            dconv = spread_ref[at, :] * (
                ds
                - jnp.mean(ds, axis=-1, keepdims=True)
                - scaled * jnp.mean(ds * scaled, axis=-1, keepdims=True)
            )
            dconv_ref[i] = dconv
            return (
                sums[0] + jnp.sum(dconv, axis=0, keepdims=True),
                sums[1] + jnp.sum(dn * scaled, axis=0, keepdims=True),
                sums[2] + jnp.sum(dn, axis=0, keepdims=True),
            )

        sums = lax.fori_loop(0, height, back, (zero, zero, zero))

        def tap_column(j, _):
            for b in range(channels // 128):
                lanes = slice(b * 128, (b + 1) * 128)
                got = []
                for d in range(reach):
                    total = jnp.zeros((width, 128), F32)
                    for i in range(height):
                        total = total + shifted[j, i + d, :, lanes] * dconv_ref[i, :, lanes]
                    got.append(jnp.sum(total, axis=0, keepdims=True))
                for d in range(reach):
                    tap_grad[j, d : d + 1, lanes] = got[d]
            return 0

        lax.fori_loop(0, reach, tap_column, 0)
        small_grad[...] = jnp.zeros_like(small_grad)
        for t in range(taps):
            small_grad[t : t + 1, :] = tap_grad[t % reach, t // reach : t // reach + 1, :]
        for k, value in enumerate((*sums, bias_grad, scale_grad)):
            small_grad[CHAN_ROW + k : CHAN_ROW + k + 1, :] = value
        grad_out[step] = small_grad[...].astype(BF)
        grad_copy = push(grad_out.at[step], grad_in.at[step], pair)
        if step + 1 < STEPS:
            shift_rows(step + 1)
            small_m_copy.wait_recv()
            join(1, small_m)
        else:
            mlp_copy.wait_recv()
            mlp = mlp_ref[...] + mlp_in[...].astype(F32) + small_p[CHAN_ROW + 3 : CHAN_ROW + 4, :]
            ofeat_ref[...] = (
                image_ref[step].astype(F32) + small_p[CHAN_ROW + 4 : CHAN_ROW + 5, :] * mlp
            ).astype(BF)
        grad_copy.wait_recv()
        moment = MOMENTUM * small_m[...] + (grad_out[step].astype(F32) + grad_in[step].astype(F32))
        small_m[...] = moment
        stepped = small_p[...] - RATE * moment
        gossip_small_out[step] = stepped.astype(BF)
        small_gossip = push(gossip_small_out.at[step], gossip_small_in.at[step], onward)
        if step + 1 < STEPS:
            m_copy.wait_recv()
            m_in_full[their_rows, :] = m_theirs[...].astype(F32)
            w_in_full[their_rows, :] = w_in_low[0, their_rows, :].astype(F32)
            for c in range(hid // CUT):
                in_update(step, c, in_grad[:, c * CUT : (c + 1) * CUT])
            cot_copy = push(cot_ref.at[step + 1], cot_theirs.at[step + 1], pair)
        if not final:
            small_gossip.wait_recv()
            small_p[...] = 0.5 * (stepped + gossip_small_in[step].astype(F32))

    last = STEPS - 1
    last_copies = []
    for c, copy in enumerate(gossip["in"]):
        cut = slice(c * CUT, (c + 1) * CUT)
        cols = pl.ds(pl.multiple_of(grp * hid + c * CUT, CUT), CUT)
        copy.wait_recv()
        last_send[c] = (
            0.5 * (w_in_full[their_rows, cut] + q_in_recv[last, c, their_rows, :].astype(F32))
        ).astype(BF)
        last_copies.append(push(last_send.at[c], last_recv.at[c], pair))
        oin_ref[:, cols] = 0.5 * (w_in_full[my_rows, cut] + q_in_recv[last, c, my_rows, :].astype(F32))
    gossip["bias"].wait_recv()
    obin_ref[...] = 0.5 * (bias_p[...] + bias_in[last, 0:1, :])
    for c, copy in enumerate(last_copies):
        cols = pl.ds(pl.multiple_of(other * hid + c * CUT, CUT), CUT)
        copy.wait_recv()
        oin_ref[:, cols] = last_recv[c].astype(F32)
    for c, copy in enumerate(gossip["out"]):
        cut = slice(c * CUT, (c + 1) * CUT)
        copy.wait_recv()
        oout_ref[cut, :] = 0.5 * (w_out_full[cut, :] + q_out_recv[last, cut, :].astype(F32))
    small_gossip.wait_recv()
    small_p[...] = 0.5 * (stepped + gossip_small_in[last].astype(F32))

    def mine_of(value):
        return jnp.where(grp == 0, value[:, 0:half], value[:, half:])

    okernel_ref[:, 0, :] = mine_of(small_p[0:taps, :])
    ochan_ref[:, 0, :] = mine_of(small_p[CHAN_ROW : CHAN_ROW + 5, :])
    for copy in started:
        copy.wait_send()


def write_results(*refs):
    sems = refs[-1]
    half = (len(refs) - 1) // 2
    copies = [
        pltpu.make_async_copy(src, dst, sems.at[k])
        for k, (src, dst) in enumerate(zip(refs[:half], refs[half:-1]))
    ]
    for copy in copies:
        copy.start()
    for copy in copies:
        copy.wait()


def fused_device(
    images, cotangent, dw_kernel, chan_vec, w_in, b_in, w_out,
    mom_kernel, mom_chan, mom_in, mom_bin, mom_out,
):
    steps, _, _, height, width, channels = images.shape
    rows = height * width
    taps, half = dw_kernel.shape[1:]
    reach = math.isqrt(taps)
    margin = reach // 2
    hid = b_in.shape[1]
    V = pltpu.VMEM
    scratch = [
        V((2, SMALL_ROWS, half), F32), V((2, SMALL_ROWS, half), F32),
        V((SMALL_ROWS, channels), F32), V((SMALL_ROWS, channels), F32),
        V((reach, height + 2 * margin, width, channels), F32),
        V((rows, channels), F32), V((rows, 1), F32),
        V((steps, 2 * rows, channels), BF), V((steps, rows, channels), BF),
        V((2 * rows, channels), BF), V((2 * rows, hid), BF), V((2 * rows, hid), BF),
        V((rows, channels), F32), V((rows, channels), BF), V((rows, channels), BF),
        V((rows, channels), F32), V((steps, rows, channels), BF), V((steps, rows, channels), BF),
        V((height, width, channels), F32), V((reach, 8, channels), F32),
        V((SMALL_ROWS, channels), F32),
        V((steps, SMALL_ROWS, channels), BF), V((steps, SMALL_ROWS, channels), BF),
        V((steps, SMALL_ROWS, channels), BF), V((steps, SMALL_ROWS, channels), BF),
        V((1, hid), F32), V((1, hid), F32),
        V((steps, 8, hid), F32), V((steps, 8, hid), F32), V((1, hid), F32),
        V((half, hid), BF), V((half, hid), BF), V((half, hid), BF),
        V((steps, channels, hid), BF), V((channels, hid), F32), V((channels, hid), F32),
        V((steps, hid, channels), BF), V((hid, channels), F32), V((hid, channels), F32),
        V((steps, hid, channels), BF), V((steps, hid, channels), BF),
        V((steps, hid // CUT, channels, CUT), BF), V((steps, hid // CUT, channels, CUT), BF),
        V((hid // CUT, half, CUT), BF), V((hid // CUT, half, CUT), BF),
        V((channels, 2 * rows), BF), V((channels, hid), F32), V((half, 2 * hid), F32),
        pltpu.SemaphoreType.DMA((48,)), pltpu.SemaphoreType.DMA((48,)),
        pltpu.SemaphoreType.DMA((3,)),
    ]
    shapes = [
        jax.ShapeDtypeStruct((taps, 1, half), F32),
        jax.ShapeDtypeStruct((chan_vec.shape[1], 1, half), F32),
        jax.ShapeDtypeStruct(w_in.shape[1:], F32),
        jax.ShapeDtypeStruct((1, hid), F32),
        jax.ShapeDtypeStruct(w_out.shape[1:], F32),
        jax.ShapeDtypeStruct((rows, channels), BF),
    ]
    whole = pl.BlockSpec(memory_space=pltpu.VMEM)
    left = pl.BlockSpec(memory_space=pl.ANY)

    def rows_apart(value):
        return value.transpose(1, 0, 2)

    out = pl.pallas_call(
        lambda *refs: fused_kernel((height, width, channels, hid), *refs),
        out_shape=shapes,
        in_specs=[whole] * 6 + [left] + [whole] * 2 + [left, whole, left],
        out_specs=[whole] * 6,
        scratch_shapes=scratch,
        compiler_params=pltpu.CompilerParams(
            collective_id=0, has_side_effects=True, vmem_limit_bytes=56 * 2**20
        ),
    )(
        images.reshape(steps, rows, channels), cotangent.reshape(steps, rows, channels),
        rows_apart(dw_kernel), rows_apart(chan_vec), w_in[0], b_in, w_out[0],
        rows_apart(mom_kernel), rows_apart(mom_chan), mom_in[0], mom_bin, mom_out[0],
    )
    out = pl.pallas_call(
        write_results,
        out_shape=shapes,
        in_specs=[pl.BlockSpec(memory_space=pltpu.HBM)] * 6,
        out_specs=[pl.BlockSpec(memory_space=pltpu.HBM)] * 6,
        scratch_shapes=[pltpu.SemaphoreType.DMA((6,))],
        compiler_params=pltpu.CompilerParams(vmem_limit_bytes=60 * 2**20),
    )(*out)
    return (
        rows_apart(out[0]), rows_apart(out[1]), out[2][None], out[3], out[4][None],
        out[5].reshape(1, 1, height, width, channels),
    )


def solution(mesh):
    fused = mesh.shape["grp"] == 2 and mesh.shape["peer"] > 4
    return jax.shard_map(
        fused_device if fused else per_device,
        mesh=mesh,
        in_specs=(
            P(None, "peer", "grp", None, None, None),
            P(None, "peer", "grp", None, None, None),
            P("peer", None, "grp"),
            P("peer", None, "grp"),
            P("peer", "grp", None),
            P("peer", "grp"),
            P("peer", "grp", None),
            P("peer", None, "grp"),
            P("peer", None, "grp"),
            P("peer", "grp", None),
            P("peer", "grp"),
            P("peer", "grp", None),
        ),
        out_specs=(
            P("peer", None, "grp"),
            P("peer", None, "grp"),
            P("peer", "grp", None),
            P("peer", "grp"),
            P("peer", "grp", None),
            P("peer", "grp", None, None, None),
        ),
        check_vma=False,
    )
```

```python
import math

import jax
import jax.numpy as jnp
from jax import lax
from jax.experimental import pallas as pl
from jax.experimental.pallas import tpu as pltpu
from jax.sharding import PartitionSpec as P

STEPS = 2


EPS = 1e-06
MOMENTUM = 0.9
RATE = 0.0005
SQRT_HALF = 0.7071067811865476
INV_ROOT_TWO_PI = 0.3989422804014327


def passed_along(block, axis, distance):
    devices = range(lax.axis_size(axis))
    route = [((i - distance) % len(devices), i) for i in devices]
    return lax.ppermute(block, axis, route)


def depthwise(field, kernel):
    channels = kernel.shape[-1]
    reach = math.isqrt(kernel.shape[0])
    margin = reach // 2
    filter_taps = kernel.reshape(reach, reach, 1, channels)
    return lax.conv_general_dilated(
        field,
        filter_taps,
        (1, 1),
        ((margin, margin), (margin, margin)),
        dimension_numbers=("NHWC", "HWIO", "NHWC"),
        feature_group_count=channels,
        precision=lax.Precision.HIGHEST,
    )


def gelu_value(value):
    return 0.5 * value * (1.0 + lax.erf(value * SQRT_HALF))


def gelu_slope(value):
    return (
        0.5 * (1.0 + lax.erf(value * SQRT_HALF))
        + value * jnp.exp(-0.5 * value * value) * INV_ROOT_TWO_PI
    )


def channel_front(image, kernel, chan):
    height, width, channels = image.shape
    field = image.astype(jnp.float32)[None]
    conv = depthwise(field, kernel)[0].reshape(height * width, channels) + chan[0]
    center = conv - jnp.mean(conv, axis=-1, keepdims=True)
    spread = lax.rsqrt(jnp.mean(center * center, axis=-1, keepdims=True) + EPS)
    scaled = center * spread
    normed = (scaled * chan[1] + chan[2]).astype(jnp.bfloat16)
    return (field, scaled, spread, normed)


def channel_back(field, scaled, spread, dnormed, chan, kernel, bias_grad, scale_grad):
    d_gain = jnp.sum(dnormed * scaled, axis=0)
    d_shift = jnp.sum(dnormed, axis=0)
    dscaled = dnormed * chan[1]
    dconv = spread * (
        dscaled
        - jnp.mean(dscaled, axis=-1, keepdims=True)
        - scaled * jnp.mean(dscaled * scaled, axis=-1, keepdims=True)
    )
    d_bias = jnp.sum(dconv, axis=0)
    _, pullback = jax.vjp(lambda taps: depthwise(field, taps), kernel)
    (d_kernel,) = pullback(dconv.reshape(field.shape))
    d_chan = jnp.stack([d_bias, d_gain, d_shift, bias_grad, scale_grad])
    return (d_kernel, d_chan)


def per_device(
    images,
    cotangent,
    dw_kernel,
    chan_vec,
    w_in,
    b_in,
    w_out,
    mom_kernel,
    mom_chan,
    mom_in,
    mom_bin,
    mom_out,
):
    params = (dw_kernel[0], chan_vec[0], w_in[0], b_in[0], w_out[0])
    moments = (mom_kernel[0], mom_chan[0], mom_in[0], mom_bin[0], mom_out[0])
    features = None
    for round_index in range(STEPS):
        kernel, chan, bias_in = (
            lax.all_gather(params[0], "grp", axis=1, tiled=True),
            lax.all_gather(params[1], "grp", axis=1, tiled=True),
            lax.all_gather(params[3], "grp", axis=0, tiled=True),
        )
        in_shard = params[2].astype(jnp.bfloat16)
        out_shard = params[4].astype(jnp.bfloat16)
        image = images[round_index, 0, 0]
        height, width, channels = image.shape
        rows = height * width
        field, scaled, spread, normed = channel_front(image, kernel, chan)
        w_in_full, w_out_full = (
            lax.all_gather(in_shard, "grp", axis=0, tiled=True),
            lax.all_gather(out_shard, "grp", axis=0, tiled=True),
        )
        pre = jnp.dot(normed, w_in_full, preferred_element_type=jnp.float32) + bias_in
        hidden = gelu_value(pre).astype(jnp.bfloat16)
        mlp = jnp.dot(hidden, w_out_full, preferred_element_type=jnp.float32) + chan[3]
        features = (image.reshape(rows, channels).astype(jnp.float32) + chan[4] * mlp).astype(
            jnp.bfloat16
        )
        cot = cotangent[round_index, 0, 0].reshape(rows, channels).astype(jnp.float32)
        bias_grad = jnp.sum(cot * chan[4], axis=0)
        scale_grad = jnp.sum(cot * mlp, axis=0)
        dmlp = (cot * chan[4]).astype(jnp.bfloat16)
        g_out = jnp.dot(hidden.T, dmlp, preferred_element_type=jnp.float32)
        dhid = jnp.dot(dmlp, w_out_full.T, preferred_element_type=jnp.float32)
        dpre = (dhid * gelu_slope(pre)).astype(jnp.bfloat16)
        g_bin = jnp.sum(dpre.astype(jnp.float32), axis=0)
        g_in = jnp.dot(normed.T, dpre, preferred_element_type=jnp.float32)
        dnormed = jnp.dot(dpre, w_in_full.T, preferred_element_type=jnp.float32)
        d_kernel, d_chan = channel_back(
            field, scaled, spread, dnormed, chan, kernel, bias_grad, scale_grad
        )
        sum_kernel, sum_chan, sum_in, sum_bin, sum_out = (
            lax.psum_scatter(
                d_kernel.astype(jnp.bfloat16), "grp", scatter_dimension=1, tiled=True
            ).astype(jnp.float32),
            lax.psum_scatter(
                d_chan.astype(jnp.bfloat16), "grp", scatter_dimension=1, tiled=True
            ).astype(jnp.float32),
            lax.psum_scatter(
                g_in.astype(jnp.bfloat16), "grp", scatter_dimension=0, tiled=True
            ).astype(jnp.float32),
            lax.psum_scatter(
                g_bin.astype(jnp.bfloat16), "grp", scatter_dimension=0, tiled=True
            ).astype(jnp.float32),
            lax.psum_scatter(
                g_out.astype(jnp.bfloat16), "grp", scatter_dimension=0, tiled=True
            ).astype(jnp.float32),
        )
        summed = (sum_kernel, sum_chan, sum_in, sum_bin, sum_out)
        moments = tuple((MOMENTUM * old + grad for old, grad in zip(moments, summed)))
        stepped = tuple((value - RATE * moment for value, moment in zip(params, moments)))
        partner = passed_along(
            (stepped[0], stepped[1], stepped[2], stepped[3], stepped[4]), "peer", 2**round_index
        )
        params = tuple((0.5 * (mine + theirs) for mine, theirs in zip(stepped, partner)))
    return (
        params[0][None],
        params[1][None],
        params[2][None],
        params[3][None],
        params[4][None],
        features.reshape(1, 1, height, width, channels),
    )


BF = jnp.bfloat16
F32 = jnp.float32
CHAN_ROW = 56
SMALL_ROWS = 64
CUT = 256
DEVICE = pl.DeviceIdType.MESH


def dot(a, b, over_a=1, over_b=0):
    return lax.dot_general(
        a, b, (((over_a,), (over_b,)), ((), ())), preferred_element_type=F32
    )


def fused_kernel(
    shape,
    image_ref, cot_ref, kernel_ref, chan_ref, win_ref, bin_ref, wout_ref,
    mkernel_ref, mchan_ref, min_ref, mbin_ref, mout_ref,
    okernel_ref, ochan_ref, oin_ref, obin_ref, oout_ref, ofeat_ref,
    small_mine, small_theirs, small_p, small_m, shifted, scaled_ref, spread_ref,
    normed, cot_theirs, dmlp, hidden, dpre, mlp_ref, mlp_out, mlp_in,
    dnorm_mine, dnorm_out, dnorm_in, dconv_ref, tap_grad, small_grad, grad_out, grad_in,
    gossip_small_out, gossip_small_in, bias_p, bias_m, bias_out, bias_in, bias_grad_ref,
    w_stage, m_stage, m_theirs, w_in_low, w_in_full, m_in_full, w_out_low, w_out_full, m_out_full,
    q_out_send, q_out_recv, q_in_send, q_in_recv, last_send, last_recv,
    normed_t, in_grad, m_in_rows, send_sem, recv_sem, load_sem,
):
    height, width, channels, hid = shape
    rows = height * width
    half = channels // 2
    reach = math.isqrt(kernel_ref.shape[0])
    margin = reach // 2
    taps = reach * reach
    peers = lax.axis_size("peer")
    me = lax.axis_index("peer")
    grp = lax.axis_index("grp")
    other = 1 - grp
    pair = (me, other)

    barrier = pltpu.get_barrier_semaphore()
    pl.semaphore_signal(barrier, inc=1, device_id=pair, device_id_type=DEVICE)
    for step in range(STEPS):
        source = (lax.rem(me + peers - 2**step, peers), grp)
        pl.semaphore_signal(barrier, inc=1, device_id=source, device_id_type=DEVICE)

    loads = [
        pltpu.make_async_copy(src, dst, load_sem.at[k])
        for k, (src, dst) in enumerate(
            ((wout_ref, w_out_full), (mout_ref, m_out_full), (min_ref, m_in_rows))
        )
    ]
    for load in loads:
        load.start()
    started = []

    def push(src, dst, device):
        at = len(started)
        copy = pltpu.make_async_remote_copy(
            src_ref=src, dst_ref=dst, send_sem=send_sem.at[at], recv_sem=recv_sem.at[at],
            device_id=device, device_id_type=DEVICE,
        )
        copy.start()
        started.append(copy)
        return copy

    my_rows = pl.ds(pl.multiple_of(grp * half, 16), half)
    their_rows = pl.ds(pl.multiple_of(other * half, 16), half)
    my_cols = pl.ds(pl.multiple_of(grp * hid, 128), hid)
    their_cols = pl.ds(pl.multiple_of(other * hid, 128), hid)

    small_mine[...] = jnp.zeros_like(small_mine)
    small_mine[0, 0:taps, :] = kernel_ref[:, 0, :]
    small_mine[0, CHAN_ROW : CHAN_ROW + 5, :] = chan_ref[:, 0, :]
    w_stage[...] = win_ref[:, their_cols].astype(BF)
    pl.semaphore_wait(barrier, 1 + STEPS)
    small_copy = push(small_mine.at[0], small_theirs.at[0], pair)
    cuts = [slice(c * CUT, (c + 1) * CUT) for c in range(hid // CUT)]
    early = len(cuts) - 1
    w_copies = [
        push(w_stage.at[:, cut], w_in_low.at[0, my_rows, cut], pair) for cut in cuts[:early]
    ]
    small_mine[1, 0:taps, :] = mkernel_ref[:, 0, :]
    small_mine[1, CHAN_ROW : CHAN_ROW + 5, :] = mchan_ref[:, 0, :]

    w_in_low[0, my_rows, :] = win_ref[:, my_cols].astype(BF)
    w_in_full[my_rows, :] = win_ref[:, my_cols]
    bias_p[...] = bin_ref[...]
    bias_m[...] = mbin_ref[...]

    def shift_rows(step):
        shifted[:, 0:margin] = jnp.zeros((reach, margin, width, channels), F32)
        shifted[:, margin + height :] = jnp.zeros((reach, margin, width, channels), F32)
        column = lax.broadcasted_iota(jnp.int32, (width, channels), 0)

        def body(i, _):
            x = image_ref[step, pl.ds(pl.multiple_of(i * width, width), width), :].astype(F32)
            for j in range(reach):
                off = j - margin
                moved = x if off == 0 else pltpu.roll(x, (-off) % width, 0)
                inside = (column + off >= 0) & (column + off < width)
                shifted[j, i + margin] = jnp.where(inside, moved, 0.0)
            return 0

        lax.fori_loop(0, height, body, 0)

    def front(step):
        bias, gain, shift = (small_p[CHAN_ROW + k : CHAN_ROW + k + 1, :] for k in range(3))

        def body(i, _):
            conv = jnp.zeros((width, channels), F32)
            for t in range(taps):
                conv = conv + shifted[t % reach, i + t // reach] * small_p[t : t + 1, :]
            conv = conv + bias
            center = conv - jnp.mean(conv, axis=-1, keepdims=True)
            spread = lax.rsqrt(jnp.mean(center * center, axis=-1, keepdims=True) + EPS)
            scaled = center * spread
            at = pl.ds(pl.multiple_of(i * width, width), width)
            scaled_ref[at, :] = scaled
            spread_ref[at, :] = spread
            normed[step, at, :] = (scaled * gain + shift).astype(BF)
            return 0

        copies = []
        for h in range(2):
            lax.fori_loop(h * height // 2, (h + 1) * height // 2, body, 0)
            at = slice(h * rows // 2, (h + 1) * rows // 2)
            theirs = slice(rows + at.start, rows + at.stop)
            copies.append(push(normed.at[step, at], normed.at[step, theirs], pair))
        return copies

    def begin(step, place):
        at = slice(place * rows, (place + 1) * rows)
        scale = small_p[CHAN_ROW + 4 : CHAN_ROW + 5, :]
        cot = (cot_ref[step] if place == 0 else cot_theirs[step]).astype(F32)
        dmlp[at, :] = (cot * scale).astype(BF)
        return cot, at

    def chunk(step, at, c):
        cut = slice(c * CUT, (c + 1) * CUT)
        pre = dot(normed[step, at, :], w_in_low[step, :, cut]) + bias_p[0:1, cut]
        bell = 0.5 * (1.0 + lax.erf(pre * SQRT_HALF))
        hidden[at, cut] = (pre * bell).astype(BF)
        slope = bell + pre * jnp.exp(-0.5 * pre * pre) * INV_ROOT_TWO_PI
        dhid = dot(dmlp[at, :], w_out_low[step, cut, :], 1, 1)
        dpre[at, cut] = (dhid * slope).astype(BF)

    def in_update(step, c, grad):
        cut = slice(c * CUT, (c + 1) * CUT)
        moment = MOMENTUM * m_in_full[:, cut] + grad
        m_in_full[:, cut] = moment
        stepped = w_in_full[:, cut] - RATE * moment
        w_in_full[:, cut] = stepped
        q_in_send[step, c] = stepped.astype(BF)
        gossip["in"].append(push(q_in_send.at[step, c], q_in_recv.at[step, c], onward))

    def in_gradient(step, c):
        return dot(normed_t[...], dpre[:, c * CUT : (c + 1) * CUT])

    def out_updates(step):
        for c in range(hid // CUT):
            cut = slice(c * CUT, (c + 1) * CUT)
            grad = dot(hidden[:, cut], dmlp[...], 0, 0)
            moment = MOMENTUM * m_out_full[cut, :] + grad
            m_out_full[cut, :] = moment
            stepped = w_out_full[cut, :] - RATE * moment
            w_out_full[cut, :] = stepped
            q_out_send[step, cut, :] = stepped.astype(BF)
            gossip["out"].append(push(q_out_send.at[step, cut], q_out_recv.at[step, cut], onward))

    def bias_update(step):
        bias_moment = MOMENTUM * bias_m[...] + jnp.sum(dpre[...].astype(F32), axis=0, keepdims=True)
        bias_m[...] = bias_moment
        bias_p[...] = bias_p[...] - RATE * bias_moment
        bias_out[step] = jnp.broadcast_to(bias_p[...], bias_out.shape[1:])
        gossip["bias"] = push(bias_out.at[step], bias_in.at[step], onward)

    shift_rows(0)

    def join(k, full):
        mine, theirs = small_mine[k], small_theirs[k]
        first = jnp.where(grp == 0, mine, theirs)
        second = jnp.where(grp == 0, theirs, mine)
        full[...] = jnp.concatenate([first, second], axis=1)

    small_copy.wait_recv()
    join(0, small_p)

    for step in range(STEPS):
        normed_copies = front(step)
        if step == 0:
            cot_copy = push(cot_ref.at[0], cot_theirs.at[0], pair)
            loads[0].wait()
            w_out_low[0] = w_out_full[...].astype(BF)
            for cut in cuts[early:]:
                w_copies.append(push(w_stage.at[:, cut], w_in_low.at[0, my_rows, cut], pair))
            loads[2].wait()
            m_in_full[my_rows, :] = m_in_rows[:, my_cols]
            m_stage[...] = m_in_rows[:, their_cols].astype(BF)
            m_copies = [push(m_stage.at[:, cut], m_theirs.at[:, cut], pair) for cut in cuts[:-1]]
            w_copies[0].wait_recv()
        else:
            for c, copy in enumerate(gossip["out"]):
                cut = slice(c * CUT, (c + 1) * CUT)
                copy.wait_recv()
                value = 0.5 * (w_out_full[cut, :] + q_out_recv[0, cut, :].astype(F32))
                w_out_full[cut, :] = value
                w_out_low[1, cut, :] = value.astype(BF)
            for c, copy in enumerate(gossip["in"]):
                cut = slice(c * CUT, (c + 1) * CUT)
                copy.wait_recv()
                value = 0.5 * (w_in_full[:, cut] + q_in_recv[0, c].astype(F32))
                w_in_full[:, cut] = value
                w_in_low[1, :, cut] = value.astype(BF)
            gossip["bias"].wait_recv()
            bias_p[...] = 0.5 * (bias_p[...] + bias_in[0, 0:1, :])
        onward = (lax.rem(me + 2**step, peers), grp)
        gossip = {"out": [], "in": []}

        other_at = slice(rows, 2 * rows)

        def meet():
            for copy in normed_copies:
                copy.wait_recv()
            normed_t[:, other_at] = normed[step, other_at, :].T
            cot_copy.wait_recv()
            return begin(step, 1)

        cot, at = begin(step, 0)
        chunk(step, at, 0)
        if step == 0:
            normed_t[:, at] = normed[step, at, :].T
            other_cot, _ = meet()
            chunk(step, other_at, 0)
        for c in range(1, len(cuts)):
            if step == 0:
                w_copies[c].wait_recv()
            chunk(step, at, c)
            if step == 0:
                chunk(step, other_at, c)
        final = step == STEPS - 1
        if step == 0:
            dnorm_out[step] = dot(dpre[other_at, :], w_in_low[step], 1, 1).astype(BF)
            dnorm_copy = push(dnorm_out.at[step], dnorm_in.at[step], pair)
            m_copies.append(push(m_stage.at[:, cuts[-1]], m_theirs.at[:, cuts[-1]], pair))
            small_m_copy = push(small_mine.at[1], small_theirs.at[1], pair)
        dnorm_mine[...] = dot(dpre[at, :], w_in_low[step], 1, 1)
        mlp = dot(hidden[at, :], w_out_low[step])
        mlp_ref[...] = mlp
        if step > 0:
            normed_t[:, at] = normed[step, at, :].T
        scale_grad = jnp.sum(cot * mlp, axis=0, keepdims=True)
        cot_sum = jnp.sum(cot, axis=0, keepdims=True)
        scale_grad = scale_grad + cot_sum * small_p[CHAN_ROW + 3 : CHAN_ROW + 4, :]
        bias_grad = jnp.sum(cot * small_p[CHAN_ROW + 4 : CHAN_ROW + 5, :], axis=0, keepdims=True)
        if step == 0:
            loads[1].wait()
            w_in_full[their_rows, :] = w_in_low[0, their_rows, :].astype(F32)
        else:
            other_cot, _ = meet()
            for c in range(len(cuts)):
                chunk(step, other_at, c)
                if final:
                    in_update(step, c, in_gradient(step, c))
            dnorm_out[step] = dot(dpre[other_at, :], w_in_low[step], 1, 1).astype(BF)
            dnorm_copy = push(dnorm_out.at[step], dnorm_in.at[step], pair)
        out_updates(step)
        mlp = dot(hidden[other_at, :], w_out_low[step])
        scale_grad = scale_grad + jnp.sum(other_cot * mlp, axis=0, keepdims=True)
        bias_update(step)
        if final:
            mlp_out[...] = mlp.astype(BF)
        else:
            for c, cut in enumerate(cuts):
                if c == len(cuts) - 1:
                    in_grad[:, cut] = in_gradient(step, c)
                else:
                    m_copies[c].wait_recv()
                    m_in_full[their_rows, cut] = m_theirs[:, cut].astype(F32)
                    in_update(step, c, in_gradient(step, c))

        dnorm_copy.wait_recv()
        if final:
            mlp_copy = push(mlp_out, mlp_in, pair)
        gain = small_p[CHAN_ROW + 1 : CHAN_ROW + 2, :]
        zero = jnp.zeros((1, channels), F32)

        def back(i, sums):
            at = pl.ds(pl.multiple_of(i * width, width), width)
            dn = dnorm_mine[at, :] + dnorm_in[step, at, :].astype(F32)
            scaled = scaled_ref[at, :]
            ds = dn * gain
            dconv = spread_ref[at, :] * (
                ds
                - jnp.mean(ds, axis=-1, keepdims=True)
                - scaled * jnp.mean(ds * scaled, axis=-1, keepdims=True)
            )
            dconv_ref[i] = dconv
            return (
                sums[0] + jnp.sum(dconv, axis=0, keepdims=True),
                sums[1] + jnp.sum(dn * scaled, axis=0, keepdims=True),
                sums[2] + jnp.sum(dn, axis=0, keepdims=True),
            )

        sums = lax.fori_loop(0, height, back, (zero, zero, zero))

        def tap_column(j, _):
            for b in range(channels // 128):
                lanes = slice(b * 128, (b + 1) * 128)
                got = []
                for d in range(reach):
                    total = jnp.zeros((width, 128), F32)
                    for i in range(height):
                        total = total + shifted[j, i + d, :, lanes] * dconv_ref[i, :, lanes]
                    got.append(jnp.sum(total, axis=0, keepdims=True))
                for d in range(reach):
                    tap_grad[j, d : d + 1, lanes] = got[d]
            return 0

        lax.fori_loop(0, reach, tap_column, 0)
        small_grad[...] = jnp.zeros_like(small_grad)
        for t in range(taps):
            small_grad[t : t + 1, :] = tap_grad[t % reach, t // reach : t // reach + 1, :]
        for k, value in enumerate((*sums, bias_grad, scale_grad)):
            small_grad[CHAN_ROW + k : CHAN_ROW + k + 1, :] = value
        grad_out[step] = small_grad[...].astype(BF)
        grad_copy = push(grad_out.at[step], grad_in.at[step], pair)
        if step + 1 < STEPS:
            shift_rows(step + 1)
            small_m_copy.wait_recv()
            join(1, small_m)
        else:
            mlp_copy.wait_recv()
            mlp = mlp_ref[...] + mlp_in[...].astype(F32) + small_p[CHAN_ROW + 3 : CHAN_ROW + 4, :]
            ofeat_ref[...] = (
                image_ref[step].astype(F32) + small_p[CHAN_ROW + 4 : CHAN_ROW + 5, :] * mlp
            ).astype(BF)
        grad_copy.wait_recv()
        moment = MOMENTUM * small_m[...] + (grad_out[step].astype(F32) + grad_in[step].astype(F32))
        small_m[...] = moment
        stepped = small_p[...] - RATE * moment
        gossip_small_out[step] = stepped.astype(BF)
        small_gossip = push(gossip_small_out.at[step], gossip_small_in.at[step], onward)
        if step + 1 < STEPS:
            m_copies[-1].wait_recv()
            m_in_full[their_rows, cuts[-1]] = m_theirs[:, cuts[-1]].astype(F32)
            in_update(step, len(cuts) - 1, in_grad[:, cuts[-1]])
            cot_copy = push(cot_ref.at[step + 1], cot_theirs.at[step + 1], pair)
        if not final:
            small_gossip.wait_recv()
            small_p[...] = 0.5 * (stepped + gossip_small_in[step].astype(F32))

    last = STEPS - 1
    last_copies = []
    for c, copy in enumerate(gossip["in"]):
        cut = slice(c * CUT, (c + 1) * CUT)
        cols = pl.ds(pl.multiple_of(grp * hid + c * CUT, CUT), CUT)
        copy.wait_recv()
        last_send[c] = (
            0.5 * (w_in_full[their_rows, cut] + q_in_recv[last, c, their_rows, :].astype(F32))
        ).astype(BF)
        last_copies.append(push(last_send.at[c], last_recv.at[c], pair))
        oin_ref[:, cols] = 0.5 * (w_in_full[my_rows, cut] + q_in_recv[last, c, my_rows, :].astype(F32))
    gossip["bias"].wait_recv()
    obin_ref[...] = 0.5 * (bias_p[...] + bias_in[last, 0:1, :])
    for c, copy in enumerate(last_copies):
        cols = pl.ds(pl.multiple_of(other * hid + c * CUT, CUT), CUT)
        copy.wait_recv()
        oin_ref[:, cols] = last_recv[c].astype(F32)
    for c, copy in enumerate(gossip["out"]):
        cut = slice(c * CUT, (c + 1) * CUT)
        copy.wait_recv()
        oout_ref[cut, :] = 0.5 * (w_out_full[cut, :] + q_out_recv[last, cut, :].astype(F32))
    small_gossip.wait_recv()
    small_p[...] = 0.5 * (stepped + gossip_small_in[last].astype(F32))

    def mine_of(value):
        return jnp.where(grp == 0, value[:, 0:half], value[:, half:])

    okernel_ref[:, 0, :] = mine_of(small_p[0:taps, :])
    ochan_ref[:, 0, :] = mine_of(small_p[CHAN_ROW : CHAN_ROW + 5, :])
    for copy in started:
        copy.wait_send()


def write_results(*refs):
    count = (len(refs) - 2) // 3
    srcs, dsts, holds = refs[:count], refs[count : 2 * count], refs[2 * count : 3 * count]
    read_sem, write_sem = refs[-2:]
    reads = [pltpu.make_async_copy(a, b, read_sem.at[k]) for k, (a, b) in enumerate(zip(srcs, holds))]
    writes = [pltpu.make_async_copy(a, b, write_sem.at[k]) for k, (a, b) in enumerate(zip(holds, dsts))]
    for read in reads:
        read.start()
    for read, write in zip(reads, writes):
        read.wait()
        write.start()
    for write in writes:
        write.wait()


def fused_device(
    images, cotangent, dw_kernel, chan_vec, w_in, b_in, w_out,
    mom_kernel, mom_chan, mom_in, mom_bin, mom_out,
):
    steps, _, _, height, width, channels = images.shape
    rows = height * width
    taps, half = dw_kernel.shape[1:]
    reach = math.isqrt(taps)
    margin = reach // 2
    hid = b_in.shape[1]
    V = pltpu.VMEM
    scratch = [
        V((2, SMALL_ROWS, half), F32), V((2, SMALL_ROWS, half), F32),
        V((SMALL_ROWS, channels), F32), V((SMALL_ROWS, channels), F32),
        V((reach, height + 2 * margin, width, channels), F32),
        V((rows, channels), F32), V((rows, 1), F32),
        V((steps, 2 * rows, channels), BF), V((steps, rows, channels), BF),
        V((2 * rows, channels), BF), V((2 * rows, hid), BF), V((2 * rows, hid), BF),
        V((rows, channels), F32), V((rows, channels), BF), V((rows, channels), BF),
        V((rows, channels), F32), V((steps, rows, channels), BF), V((steps, rows, channels), BF),
        V((height, width, channels), F32), V((reach, 8, channels), F32),
        V((SMALL_ROWS, channels), F32),
        V((steps, SMALL_ROWS, channels), BF), V((steps, SMALL_ROWS, channels), BF),
        V((steps, SMALL_ROWS, channels), BF), V((steps, SMALL_ROWS, channels), BF),
        V((1, hid), F32), V((1, hid), F32),
        V((steps, 8, hid), F32), V((steps, 8, hid), F32), V((1, hid), F32),
        V((half, hid), BF), V((half, hid), BF), V((half, hid), BF),
        V((steps, channels, hid), BF), V((channels, hid), F32), V((channels, hid), F32),
        V((steps, hid, channels), BF), V((hid, channels), F32), V((hid, channels), F32),
        V((steps, hid, channels), BF), V((steps, hid, channels), BF),
        V((steps, hid // CUT, channels, CUT), BF), V((steps, hid // CUT, channels, CUT), BF),
        V((hid // CUT, half, CUT), BF), V((hid // CUT, half, CUT), BF),
        V((channels, 2 * rows), BF), V((channels, hid), F32), V((half, 2 * hid), F32),
        pltpu.SemaphoreType.DMA((48,)), pltpu.SemaphoreType.DMA((48,)),
        pltpu.SemaphoreType.DMA((3,)),
    ]
    shapes = [
        jax.ShapeDtypeStruct((taps, 1, half), F32),
        jax.ShapeDtypeStruct((chan_vec.shape[1], 1, half), F32),
        jax.ShapeDtypeStruct(w_in.shape[1:], F32),
        jax.ShapeDtypeStruct((1, hid), F32),
        jax.ShapeDtypeStruct(w_out.shape[1:], F32),
        jax.ShapeDtypeStruct((rows, channels), BF),
    ]
    whole = pl.BlockSpec(memory_space=pltpu.VMEM)
    left = pl.BlockSpec(memory_space=pl.ANY)

    def rows_apart(value):
        return value.transpose(1, 0, 2)

    out = pl.pallas_call(
        lambda *refs: fused_kernel((height, width, channels, hid), *refs),
        out_shape=shapes,
        in_specs=[whole] * 6 + [left] + [whole] * 2 + [left, whole, left],
        out_specs=[whole] * 6,
        scratch_shapes=scratch,
        compiler_params=pltpu.CompilerParams(
            collective_id=0, has_side_effects=True, vmem_limit_bytes=56 * 2**20
        ),
    )(
        images.reshape(steps, rows, channels), cotangent.reshape(steps, rows, channels),
        rows_apart(dw_kernel), rows_apart(chan_vec), w_in[0], b_in, w_out[0],
        rows_apart(mom_kernel), rows_apart(mom_chan), mom_in[0], mom_bin, mom_out[0],
    )
    out = pl.pallas_call(
        write_results,
        out_shape=shapes,
        in_specs=[pl.BlockSpec(memory_space=pltpu.HBM)] * 6,
        out_specs=[pl.BlockSpec(memory_space=pltpu.HBM)] * 6,
        scratch_shapes=[V(x.shape, x.dtype) for x in shapes]
        + [pltpu.SemaphoreType.DMA((6,)), pltpu.SemaphoreType.DMA((6,))],
        compiler_params=pltpu.CompilerParams(vmem_limit_bytes=60 * 2**20),
    )(*out)
    return (
        rows_apart(out[0]), rows_apart(out[1]), out[2][None], out[3], out[4][None],
        out[5].reshape(1, 1, height, width, channels),
    )


def solution(mesh):
    fused = mesh.shape["grp"] == 2 and mesh.shape["peer"] > 4
    return jax.shard_map(
        fused_device if fused else per_device,
        mesh=mesh,
        in_specs=(
            P(None, "peer", "grp", None, None, None),
            P(None, "peer", "grp", None, None, None),
            P("peer", None, "grp"),
            P("peer", None, "grp"),
            P("peer", "grp", None),
            P("peer", "grp"),
            P("peer", "grp", None),
            P("peer", None, "grp"),
            P("peer", None, "grp"),
            P("peer", "grp", None),
            P("peer", "grp"),
            P("peer", "grp", None),
        ),
        out_specs=(
            P("peer", None, "grp"),
            P("peer", None, "grp"),
            P("peer", "grp", None),
            P("peer", "grp"),
            P("peer", "grp", None),
            P("peer", "grp", None, None, None),
        ),
        check_vma=False,
    )
```

```python
import math

import jax
import jax.numpy as jnp
from jax import lax
from jax.experimental import pallas as pl
from jax.experimental.pallas import tpu as pltpu
from jax.sharding import PartitionSpec as P

STEPS = 2


EPS = 1e-06
MOMENTUM = 0.9
RATE = 0.0005
SQRT_HALF = 0.7071067811865476
INV_ROOT_TWO_PI = 0.3989422804014327


def passed_along(block, axis, distance):
    devices = range(lax.axis_size(axis))
    route = [((i - distance) % len(devices), i) for i in devices]
    return lax.ppermute(block, axis, route)


def depthwise(field, kernel):
    channels = kernel.shape[-1]
    reach = math.isqrt(kernel.shape[0])
    margin = reach // 2
    filter_taps = kernel.reshape(reach, reach, 1, channels)
    return lax.conv_general_dilated(
        field,
        filter_taps,
        (1, 1),
        ((margin, margin), (margin, margin)),
        dimension_numbers=("NHWC", "HWIO", "NHWC"),
        feature_group_count=channels,
        precision=lax.Precision.HIGHEST,
    )


def gelu_value(value):
    return 0.5 * value * (1.0 + lax.erf(value * SQRT_HALF))


def gelu_slope(value):
    return (
        0.5 * (1.0 + lax.erf(value * SQRT_HALF))
        + value * jnp.exp(-0.5 * value * value) * INV_ROOT_TWO_PI
    )


def channel_front(image, kernel, chan):
    height, width, channels = image.shape
    field = image.astype(jnp.float32)[None]
    conv = depthwise(field, kernel)[0].reshape(height * width, channels) + chan[0]
    center = conv - jnp.mean(conv, axis=-1, keepdims=True)
    spread = lax.rsqrt(jnp.mean(center * center, axis=-1, keepdims=True) + EPS)
    scaled = center * spread
    normed = (scaled * chan[1] + chan[2]).astype(jnp.bfloat16)
    return (field, scaled, spread, normed)


def channel_back(field, scaled, spread, dnormed, chan, kernel, bias_grad, scale_grad):
    d_gain = jnp.sum(dnormed * scaled, axis=0)
    d_shift = jnp.sum(dnormed, axis=0)
    dscaled = dnormed * chan[1]
    dconv = spread * (
        dscaled
        - jnp.mean(dscaled, axis=-1, keepdims=True)
        - scaled * jnp.mean(dscaled * scaled, axis=-1, keepdims=True)
    )
    d_bias = jnp.sum(dconv, axis=0)
    _, pullback = jax.vjp(lambda taps: depthwise(field, taps), kernel)
    (d_kernel,) = pullback(dconv.reshape(field.shape))
    d_chan = jnp.stack([d_bias, d_gain, d_shift, bias_grad, scale_grad])
    return (d_kernel, d_chan)


def per_device(
    images,
    cotangent,
    dw_kernel,
    chan_vec,
    w_in,
    b_in,
    w_out,
    mom_kernel,
    mom_chan,
    mom_in,
    mom_bin,
    mom_out,
):
    params = (dw_kernel[0], chan_vec[0], w_in[0], b_in[0], w_out[0])
    moments = (mom_kernel[0], mom_chan[0], mom_in[0], mom_bin[0], mom_out[0])
    features = None
    for round_index in range(STEPS):
        kernel, chan, bias_in = (
            lax.all_gather(params[0], "grp", axis=1, tiled=True),
            lax.all_gather(params[1], "grp", axis=1, tiled=True),
            lax.all_gather(params[3], "grp", axis=0, tiled=True),
        )
        in_shard = params[2].astype(jnp.bfloat16)
        out_shard = params[4].astype(jnp.bfloat16)
        image = images[round_index, 0, 0]
        height, width, channels = image.shape
        rows = height * width
        field, scaled, spread, normed = channel_front(image, kernel, chan)
        w_in_full, w_out_full = (
            lax.all_gather(in_shard, "grp", axis=0, tiled=True),
            lax.all_gather(out_shard, "grp", axis=0, tiled=True),
        )
        pre = jnp.dot(normed, w_in_full, preferred_element_type=jnp.float32) + bias_in
        hidden = gelu_value(pre).astype(jnp.bfloat16)
        mlp = jnp.dot(hidden, w_out_full, preferred_element_type=jnp.float32) + chan[3]
        features = (image.reshape(rows, channels).astype(jnp.float32) + chan[4] * mlp).astype(
            jnp.bfloat16
        )
        cot = cotangent[round_index, 0, 0].reshape(rows, channels).astype(jnp.float32)
        bias_grad = jnp.sum(cot * chan[4], axis=0)
        scale_grad = jnp.sum(cot * mlp, axis=0)
        dmlp = (cot * chan[4]).astype(jnp.bfloat16)
        g_out = jnp.dot(hidden.T, dmlp, preferred_element_type=jnp.float32)
        dhid = jnp.dot(dmlp, w_out_full.T, preferred_element_type=jnp.float32)
        dpre = (dhid * gelu_slope(pre)).astype(jnp.bfloat16)
        g_bin = jnp.sum(dpre.astype(jnp.float32), axis=0)
        g_in = jnp.dot(normed.T, dpre, preferred_element_type=jnp.float32)
        dnormed = jnp.dot(dpre, w_in_full.T, preferred_element_type=jnp.float32)
        d_kernel, d_chan = channel_back(
            field, scaled, spread, dnormed, chan, kernel, bias_grad, scale_grad
        )
        sum_kernel, sum_chan, sum_in, sum_bin, sum_out = (
            lax.psum_scatter(
                d_kernel.astype(jnp.bfloat16), "grp", scatter_dimension=1, tiled=True
            ).astype(jnp.float32),
            lax.psum_scatter(
                d_chan.astype(jnp.bfloat16), "grp", scatter_dimension=1, tiled=True
            ).astype(jnp.float32),
            lax.psum_scatter(
                g_in.astype(jnp.bfloat16), "grp", scatter_dimension=0, tiled=True
            ).astype(jnp.float32),
            lax.psum_scatter(
                g_bin.astype(jnp.bfloat16), "grp", scatter_dimension=0, tiled=True
            ).astype(jnp.float32),
            lax.psum_scatter(
                g_out.astype(jnp.bfloat16), "grp", scatter_dimension=0, tiled=True
            ).astype(jnp.float32),
        )
        summed = (sum_kernel, sum_chan, sum_in, sum_bin, sum_out)
        moments = tuple((MOMENTUM * old + grad for old, grad in zip(moments, summed)))
        stepped = tuple((value - RATE * moment for value, moment in zip(params, moments)))
        partner = passed_along(
            (stepped[0], stepped[1], stepped[2], stepped[3], stepped[4]), "peer", 2**round_index
        )
        params = tuple((0.5 * (mine + theirs) for mine, theirs in zip(stepped, partner)))
    return (
        params[0][None],
        params[1][None],
        params[2][None],
        params[3][None],
        params[4][None],
        features.reshape(1, 1, height, width, channels),
    )


BF = jnp.bfloat16
F32 = jnp.float32
CHAN_ROW = 56
SMALL_ROWS = 64
CUT = 256
DEVICE = pl.DeviceIdType.MESH


def dot(a, b, over_a=1, over_b=0):
    return lax.dot_general(
        a, b, (((over_a,), (over_b,)), ((), ())), preferred_element_type=F32
    )


def fused_kernel(
    shape,
    image_ref, cot_ref, kernel_ref, chan_ref, win_ref, bin_ref, wout_ref,
    mkernel_ref, mchan_ref, min_ref, mbin_ref, mout_ref,
    okernel_ref, ochan_ref, oin_ref, obin_ref, oout_ref, ofeat_ref,
    small_mine, small_theirs, small_p, small_m, shifted, scaled_ref, spread_ref,
    normed, cot_theirs, dmlp, hidden, dpre, mlp_ref, mlp_out, mlp_in,
    dnorm_mine, dnorm_out, dnorm_in, dconv_ref, tap_grad, small_grad, grad_out, grad_in,
    gossip_small_out, gossip_small_in, bias_p, bias_m, bias_out, bias_in, bias_grad_ref,
    w_stage, m_stage, m_theirs, w_in_low, w_in_full, m_in_full, w_out_low, w_out_full, m_out_full,
    q_out_send, q_out_recv, q_in_send, q_in_recv, last_send, last_recv,
    normed_t, in_grad, m_in_rows, send_sem, recv_sem, load_sem,
):
    height, width, channels, hid = shape
    rows = height * width
    half = channels // 2
    reach = math.isqrt(kernel_ref.shape[0])
    margin = reach // 2
    taps = reach * reach
    peers = lax.axis_size("peer")
    me = lax.axis_index("peer")
    grp = lax.axis_index("grp")
    other = 1 - grp
    pair = (me, other)

    barrier = pltpu.get_barrier_semaphore()
    pl.semaphore_signal(barrier, inc=1, device_id=pair, device_id_type=DEVICE)
    for step in range(STEPS):
        source = (lax.rem(me + peers - 2**step, peers), grp)
        pl.semaphore_signal(barrier, inc=1, device_id=source, device_id_type=DEVICE)

    loads = [
        pltpu.make_async_copy(src, dst, load_sem.at[k])
        for k, (src, dst) in enumerate(
            ((wout_ref, w_out_full), (mout_ref, m_out_full), (min_ref, m_in_rows))
        )
    ]
    for load in loads:
        load.start()
    started = []

    def push(src, dst, device):
        at = len(started)
        copy = pltpu.make_async_remote_copy(
            src_ref=src, dst_ref=dst, send_sem=send_sem.at[at], recv_sem=recv_sem.at[at],
            device_id=device, device_id_type=DEVICE,
        )
        copy.start()
        started.append(copy)
        return copy

    my_rows = pl.ds(pl.multiple_of(grp * half, 16), half)
    their_rows = pl.ds(pl.multiple_of(other * half, 16), half)
    my_cols = pl.ds(pl.multiple_of(grp * hid, 128), hid)
    their_cols = pl.ds(pl.multiple_of(other * hid, 128), hid)

    small_mine[...] = jnp.zeros_like(small_mine)
    small_mine[0, 0:taps, :] = kernel_ref[:, 0, :]
    small_mine[0, CHAN_ROW : CHAN_ROW + 5, :] = chan_ref[:, 0, :]
    w_stage[...] = win_ref[:, their_cols].astype(BF)
    pl.semaphore_wait(barrier, 1 + STEPS)
    small_copy = push(small_mine.at[0], small_theirs.at[0], pair)
    cuts = [slice(c * CUT, (c + 1) * CUT) for c in range(hid // CUT)]
    early = len(cuts) - 1
    w_copies = [
        push(w_stage.at[:, cut], w_in_low.at[0, my_rows, cut], pair) for cut in cuts[:early]
    ]
    small_mine[1, 0:taps, :] = mkernel_ref[:, 0, :]
    small_mine[1, CHAN_ROW : CHAN_ROW + 5, :] = mchan_ref[:, 0, :]

    w_in_low[0, my_rows, :] = win_ref[:, my_cols].astype(BF)
    w_in_full[my_rows, :] = win_ref[:, my_cols]
    bias_p[...] = bin_ref[...]
    bias_m[...] = mbin_ref[...]

    def shift_rows(step):
        shifted[:, 0:margin] = jnp.zeros((reach, margin, width, channels), F32)
        shifted[:, margin + height :] = jnp.zeros((reach, margin, width, channels), F32)
        column = lax.broadcasted_iota(jnp.int32, (width, channels), 0)

        def body(i, _):
            x = image_ref[step, pl.ds(pl.multiple_of(i * width, width), width), :].astype(F32)
            for j in range(reach):
                off = j - margin
                moved = x if off == 0 else pltpu.roll(x, (-off) % width, 0)
                inside = (column + off >= 0) & (column + off < width)
                shifted[j, i + margin] = jnp.where(inside, moved, 0.0)
            return 0

        lax.fori_loop(0, height, body, 0)

    def front(step):
        bias, gain, shift = (small_p[CHAN_ROW + k : CHAN_ROW + k + 1, :] for k in range(3))

        def body(i, _):
            conv = jnp.zeros((width, channels), F32)
            for t in range(taps):
                conv = conv + shifted[t % reach, i + t // reach] * small_p[t : t + 1, :]
            conv = conv + bias
            center = conv - jnp.mean(conv, axis=-1, keepdims=True)
            spread = lax.rsqrt(jnp.mean(center * center, axis=-1, keepdims=True) + EPS)
            scaled = center * spread
            at = pl.ds(pl.multiple_of(i * width, width), width)
            scaled_ref[at, :] = scaled
            spread_ref[at, :] = spread
            normed[step, at, :] = (scaled * gain + shift).astype(BF)
            return 0

        copies = []
        for h in range(4):
            lax.fori_loop(h * height // 4, (h + 1) * height // 4, body, 0)
            at = slice(h * rows // 4, (h + 1) * rows // 4)
            theirs = slice(rows + at.start, rows + at.stop)
            copies.append(push(normed.at[step, at], normed.at[step, theirs], pair))
        return copies

    def begin(step, place):
        at = slice(place * rows, (place + 1) * rows)
        scale = small_p[CHAN_ROW + 4 : CHAN_ROW + 5, :]
        cot = (cot_ref[step] if place == 0 else cot_theirs[step]).astype(F32)
        dmlp[at, :] = (cot * scale).astype(BF)
        return cot, at

    def chunk(step, at, c):
        cut = slice(c * CUT, (c + 1) * CUT)
        pre = dot(normed[step, at, :], w_in_low[step, :, cut]) + bias_p[0:1, cut]
        bell = 0.5 * (1.0 + lax.erf(pre * SQRT_HALF))
        hidden[at, cut] = (pre * bell).astype(BF)
        slope = bell + pre * jnp.exp(-0.5 * pre * pre) * INV_ROOT_TWO_PI
        dhid = dot(dmlp[at, :], w_out_low[step, cut, :], 1, 1)
        dpre[at, cut] = (dhid * slope).astype(BF)

    def in_update(step, c, grad):
        cut = slice(c * CUT, (c + 1) * CUT)
        moment = MOMENTUM * m_in_full[:, cut] + grad
        m_in_full[:, cut] = moment
        stepped = w_in_full[:, cut] - RATE * moment
        w_in_full[:, cut] = stepped
        q_in_send[step, c] = stepped.astype(BF)
        gossip["in"].append(push(q_in_send.at[step, c], q_in_recv.at[step, c], onward))

    def in_gradient(step, c):
        return dot(normed_t[...], dpre[:, c * CUT : (c + 1) * CUT])

    def out_updates(step):
        for c in range(hid // CUT):
            cut = slice(c * CUT, (c + 1) * CUT)
            grad = dot(hidden[:, cut], dmlp[...], 0, 0)
            moment = MOMENTUM * m_out_full[cut, :] + grad
            m_out_full[cut, :] = moment
            stepped = w_out_full[cut, :] - RATE * moment
            w_out_full[cut, :] = stepped
            q_out_send[step, cut, :] = stepped.astype(BF)
            gossip["out"].append(push(q_out_send.at[step, cut], q_out_recv.at[step, cut], onward))

    def bias_update(step):
        bias_moment = MOMENTUM * bias_m[...] + jnp.sum(dpre[...].astype(F32), axis=0, keepdims=True)
        bias_m[...] = bias_moment
        bias_p[...] = bias_p[...] - RATE * bias_moment
        bias_out[step] = jnp.broadcast_to(bias_p[...], bias_out.shape[1:])
        gossip["bias"] = push(bias_out.at[step], bias_in.at[step], onward)

    shift_rows(0)

    def join(k, full):
        mine, theirs = small_mine[k], small_theirs[k]
        first = jnp.where(grp == 0, mine, theirs)
        second = jnp.where(grp == 0, theirs, mine)
        full[...] = jnp.concatenate([first, second], axis=1)

    small_copy.wait_recv()
    join(0, small_p)

    for step in range(STEPS):
        normed_copies = front(step)
        if step == 0:
            cot_copy = push(cot_ref.at[0], cot_theirs.at[0], pair)
            loads[0].wait()
            w_out_low[0] = w_out_full[...].astype(BF)
            for cut in cuts[early:]:
                w_copies.append(push(w_stage.at[:, cut], w_in_low.at[0, my_rows, cut], pair))
            loads[2].wait()
            m_in_full[my_rows, :] = m_in_rows[:, my_cols]
            m_stage[...] = m_in_rows[:, their_cols].astype(BF)
            m_copies = [push(m_stage.at[:, cut], m_theirs.at[:, cut], pair) for cut in cuts[:-1]]
            w_copies[0].wait_recv()
        else:
            for c, copy in enumerate(gossip["out"]):
                cut = slice(c * CUT, (c + 1) * CUT)
                copy.wait_recv()
                value = 0.5 * (w_out_full[cut, :] + q_out_recv[0, cut, :].astype(F32))
                w_out_full[cut, :] = value
                w_out_low[1, cut, :] = value.astype(BF)
            for c, copy in enumerate(gossip["in"]):
                cut = slice(c * CUT, (c + 1) * CUT)
                copy.wait_recv()
                value = 0.5 * (w_in_full[:, cut] + q_in_recv[0, c].astype(F32))
                w_in_full[:, cut] = value
                w_in_low[1, :, cut] = value.astype(BF)
            gossip["bias"].wait_recv()
            bias_p[...] = 0.5 * (bias_p[...] + bias_in[0, 0:1, :])
        onward = (lax.rem(me + 2**step, peers), grp)
        gossip = {"out": [], "in": []}

        other_at = slice(rows, 2 * rows)

        def meet():
            for copy in normed_copies:
                copy.wait_recv()
            normed_t[:, other_at] = normed[step, other_at, :].T
            cot_copy.wait_recv()
            return begin(step, 1)

        cot, at = begin(step, 0)
        chunk(step, at, 0)
        if step == 0:
            normed_t[:, at] = normed[step, at, :].T
            other_cot, _ = meet()
            chunk(step, other_at, 0)
        for c in range(1, len(cuts)):
            if step == 0:
                w_copies[c].wait_recv()
            chunk(step, at, c)
            if step == 0:
                chunk(step, other_at, c)
        final = step == STEPS - 1
        if step == 0:
            dnorm_out[step] = dot(dpre[other_at, :], w_in_low[step], 1, 1).astype(BF)
            dnorm_copy = push(dnorm_out.at[step], dnorm_in.at[step], pair)
            m_copies.append(push(m_stage.at[:, cuts[-1]], m_theirs.at[:, cuts[-1]], pair))
            small_m_copy = push(small_mine.at[1], small_theirs.at[1], pair)
        dnorm_mine[...] = dot(dpre[at, :], w_in_low[step], 1, 1)
        mlp = dot(hidden[at, :], w_out_low[step])
        mlp_ref[...] = mlp
        if step > 0:
            normed_t[:, at] = normed[step, at, :].T
        scale_grad = jnp.sum(cot * mlp, axis=0, keepdims=True)
        cot_sum = jnp.sum(cot, axis=0, keepdims=True)
        scale_grad = scale_grad + cot_sum * small_p[CHAN_ROW + 3 : CHAN_ROW + 4, :]
        bias_grad = jnp.sum(cot * small_p[CHAN_ROW + 4 : CHAN_ROW + 5, :], axis=0, keepdims=True)
        if step == 0:
            loads[1].wait()
            w_in_full[their_rows, :] = w_in_low[0, their_rows, :].astype(F32)
        else:
            other_cot, _ = meet()
            for c in range(len(cuts)):
                chunk(step, other_at, c)
                if final:
                    in_update(step, c, in_gradient(step, c))
            dnorm_out[step] = dot(dpre[other_at, :], w_in_low[step], 1, 1).astype(BF)
            dnorm_copy = push(dnorm_out.at[step], dnorm_in.at[step], pair)
        out_updates(step)
        mlp = dot(hidden[other_at, :], w_out_low[step])
        scale_grad = scale_grad + jnp.sum(other_cot * mlp, axis=0, keepdims=True)
        bias_update(step)
        if final:
            mlp_out[...] = mlp.astype(BF)
        else:
            for c, cut in enumerate(cuts):
                if c == len(cuts) - 1:
                    in_grad[:, cut] = in_gradient(step, c)
                else:
                    m_copies[c].wait_recv()
                    m_in_full[their_rows, cut] = m_theirs[:, cut].astype(F32)
                    in_update(step, c, in_gradient(step, c))

        dnorm_copy.wait_recv()
        if final:
            mlp_copy = push(mlp_out, mlp_in, pair)
        gain = small_p[CHAN_ROW + 1 : CHAN_ROW + 2, :]
        zero = jnp.zeros((1, channels), F32)

        def back(i, sums):
            at = pl.ds(pl.multiple_of(i * width, width), width)
            dn = dnorm_mine[at, :] + dnorm_in[step, at, :].astype(F32)
            scaled = scaled_ref[at, :]
            ds = dn * gain
            dconv = spread_ref[at, :] * (
                ds
                - jnp.mean(ds, axis=-1, keepdims=True)
                - scaled * jnp.mean(ds * scaled, axis=-1, keepdims=True)
            )
            dconv_ref[i] = dconv
            return (
                sums[0] + jnp.sum(dconv, axis=0, keepdims=True),
                sums[1] + jnp.sum(dn * scaled, axis=0, keepdims=True),
                sums[2] + jnp.sum(dn, axis=0, keepdims=True),
            )

        sums = lax.fori_loop(0, height, back, (zero, zero, zero))

        def tap_column(j, _):
            for b in range(channels // 128):
                lanes = slice(b * 128, (b + 1) * 128)
                got = []
                for d in range(reach):
                    total = jnp.zeros((width, 128), F32)
                    for i in range(height):
                        total = total + shifted[j, i + d, :, lanes] * dconv_ref[i, :, lanes]
                    got.append(jnp.sum(total, axis=0, keepdims=True))
                for d in range(reach):
                    tap_grad[j, d : d + 1, lanes] = got[d]
            return 0

        lax.fori_loop(0, reach, tap_column, 0)
        small_grad[...] = jnp.zeros_like(small_grad)
        for t in range(taps):
            small_grad[t : t + 1, :] = tap_grad[t % reach, t // reach : t // reach + 1, :]
        for k, value in enumerate((*sums, bias_grad, scale_grad)):
            small_grad[CHAN_ROW + k : CHAN_ROW + k + 1, :] = value
        grad_out[step] = small_grad[...].astype(BF)
        grad_copy = push(grad_out.at[step], grad_in.at[step], pair)
        if step + 1 < STEPS:
            shift_rows(step + 1)
            small_m_copy.wait_recv()
            join(1, small_m)
        else:
            mlp_copy.wait_recv()
            mlp = mlp_ref[...] + mlp_in[...].astype(F32) + small_p[CHAN_ROW + 3 : CHAN_ROW + 4, :]
            ofeat_ref[...] = (
                image_ref[step].astype(F32) + small_p[CHAN_ROW + 4 : CHAN_ROW + 5, :] * mlp
            ).astype(BF)
        grad_copy.wait_recv()
        moment = MOMENTUM * small_m[...] + (grad_out[step].astype(F32) + grad_in[step].astype(F32))
        small_m[...] = moment
        stepped = small_p[...] - RATE * moment
        gossip_small_out[step] = stepped.astype(BF)
        small_gossip = push(gossip_small_out.at[step], gossip_small_in.at[step], onward)
        if step + 1 < STEPS:
            m_copies[-1].wait_recv()
            m_in_full[their_rows, cuts[-1]] = m_theirs[:, cuts[-1]].astype(F32)
            in_update(step, len(cuts) - 1, in_grad[:, cuts[-1]])
            cot_copy = push(cot_ref.at[step + 1], cot_theirs.at[step + 1], pair)
        if not final:
            small_gossip.wait_recv()
            small_p[...] = 0.5 * (stepped + gossip_small_in[step].astype(F32))

    last = STEPS - 1
    last_copies = []
    for c, copy in enumerate(gossip["in"]):
        cut = slice(c * CUT, (c + 1) * CUT)
        cols = pl.ds(pl.multiple_of(grp * hid + c * CUT, CUT), CUT)
        copy.wait_recv()
        last_send[c] = (
            0.5 * (w_in_full[their_rows, cut] + q_in_recv[last, c, their_rows, :].astype(F32))
        ).astype(BF)
        last_copies.append(push(last_send.at[c], last_recv.at[c], pair))
        oin_ref[:, cols] = 0.5 * (w_in_full[my_rows, cut] + q_in_recv[last, c, my_rows, :].astype(F32))
    gossip["bias"].wait_recv()
    obin_ref[...] = 0.5 * (bias_p[...] + bias_in[last, 0:1, :])
    for c, copy in enumerate(last_copies):
        cols = pl.ds(pl.multiple_of(other * hid + c * CUT, CUT), CUT)
        copy.wait_recv()
        oin_ref[:, cols] = last_recv[c].astype(F32)
    for c, copy in enumerate(gossip["out"]):
        cut = slice(c * CUT, (c + 1) * CUT)
        copy.wait_recv()
        oout_ref[cut, :] = 0.5 * (w_out_full[cut, :] + q_out_recv[last, cut, :].astype(F32))
    small_gossip.wait_recv()
    small_p[...] = 0.5 * (stepped + gossip_small_in[last].astype(F32))

    def mine_of(value):
        return jnp.where(grp == 0, value[:, 0:half], value[:, half:])

    okernel_ref[:, 0, :] = mine_of(small_p[0:taps, :])
    ochan_ref[:, 0, :] = mine_of(small_p[CHAN_ROW : CHAN_ROW + 5, :])
    for copy in started:
        copy.wait_send()


def write_results(*refs):
    count = (len(refs) - 2) // 3
    srcs, dsts, holds = refs[:count], refs[count : 2 * count], refs[2 * count : 3 * count]
    read_sem, write_sem = refs[-2:]
    reads = [pltpu.make_async_copy(a, b, read_sem.at[k]) for k, (a, b) in enumerate(zip(srcs, holds))]
    writes = [pltpu.make_async_copy(a, b, write_sem.at[k]) for k, (a, b) in enumerate(zip(holds, dsts))]
    for read in reads:
        read.start()
    for read, write in zip(reads, writes):
        read.wait()
        write.start()
    for write in writes:
        write.wait()


def fused_device(
    images, cotangent, dw_kernel, chan_vec, w_in, b_in, w_out,
    mom_kernel, mom_chan, mom_in, mom_bin, mom_out,
):
    steps, _, _, height, width, channels = images.shape
    rows = height * width
    taps, half = dw_kernel.shape[1:]
    reach = math.isqrt(taps)
    margin = reach // 2
    hid = b_in.shape[1]
    V = pltpu.VMEM
    scratch = [
        V((2, SMALL_ROWS, half), F32), V((2, SMALL_ROWS, half), F32),
        V((SMALL_ROWS, channels), F32), V((SMALL_ROWS, channels), F32),
        V((reach, height + 2 * margin, width, channels), F32),
        V((rows, channels), F32), V((rows, 1), F32),
        V((steps, 2 * rows, channels), BF), V((steps, rows, channels), BF),
        V((2 * rows, channels), BF), V((2 * rows, hid), BF), V((2 * rows, hid), BF),
        V((rows, channels), F32), V((rows, channels), BF), V((rows, channels), BF),
        V((rows, channels), F32), V((steps, rows, channels), BF), V((steps, rows, channels), BF),
        V((height, width, channels), F32), V((reach, 8, channels), F32),
        V((SMALL_ROWS, channels), F32),
        V((steps, SMALL_ROWS, channels), BF), V((steps, SMALL_ROWS, channels), BF),
        V((steps, SMALL_ROWS, channels), BF), V((steps, SMALL_ROWS, channels), BF),
        V((1, hid), F32), V((1, hid), F32),
        V((steps, 8, hid), F32), V((steps, 8, hid), F32), V((1, hid), F32),
        V((half, hid), BF), V((half, hid), BF), V((half, hid), BF),
        V((steps, channels, hid), BF), V((channels, hid), F32), V((channels, hid), F32),
        V((steps, hid, channels), BF), V((hid, channels), F32), V((hid, channels), F32),
        V((steps, hid, channels), BF), V((steps, hid, channels), BF),
        V((steps, hid // CUT, channels, CUT), BF), V((steps, hid // CUT, channels, CUT), BF),
        V((hid // CUT, half, CUT), BF), V((hid // CUT, half, CUT), BF),
        V((channels, 2 * rows), BF), V((channels, hid), F32), V((half, 2 * hid), F32),
        pltpu.SemaphoreType.DMA((48,)), pltpu.SemaphoreType.DMA((48,)),
        pltpu.SemaphoreType.DMA((3,)),
    ]
    shapes = [
        jax.ShapeDtypeStruct((taps, 1, half), F32),
        jax.ShapeDtypeStruct((chan_vec.shape[1], 1, half), F32),
        jax.ShapeDtypeStruct(w_in.shape[1:], F32),
        jax.ShapeDtypeStruct((1, hid), F32),
        jax.ShapeDtypeStruct(w_out.shape[1:], F32),
        jax.ShapeDtypeStruct((rows, channels), BF),
    ]
    whole = pl.BlockSpec(memory_space=pltpu.VMEM)
    left = pl.BlockSpec(memory_space=pl.ANY)

    def rows_apart(value):
        return value.transpose(1, 0, 2)

    out = pl.pallas_call(
        lambda *refs: fused_kernel((height, width, channels, hid), *refs),
        out_shape=shapes,
        in_specs=[whole] * 6 + [left] + [whole] * 2 + [left, whole, left],
        out_specs=[whole] * 6,
        scratch_shapes=scratch,
        compiler_params=pltpu.CompilerParams(
            collective_id=0, has_side_effects=True, vmem_limit_bytes=56 * 2**20
        ),
    )(
        images.reshape(steps, rows, channels), cotangent.reshape(steps, rows, channels),
        rows_apart(dw_kernel), rows_apart(chan_vec), w_in[0], b_in, w_out[0],
        rows_apart(mom_kernel), rows_apart(mom_chan), mom_in[0], mom_bin, mom_out[0],
    )
    out = pl.pallas_call(
        write_results,
        out_shape=shapes,
        in_specs=[pl.BlockSpec(memory_space=pltpu.HBM)] * 6,
        out_specs=[pl.BlockSpec(memory_space=pltpu.HBM)] * 6,
        scratch_shapes=[V(x.shape, x.dtype) for x in shapes]
        + [pltpu.SemaphoreType.DMA((6,)), pltpu.SemaphoreType.DMA((6,))],
        compiler_params=pltpu.CompilerParams(vmem_limit_bytes=60 * 2**20),
    )(*out)
    return (
        rows_apart(out[0]), rows_apart(out[1]), out[2][None], out[3], out[4][None],
        out[5].reshape(1, 1, height, width, channels),
    )


def solution(mesh):
    fused = mesh.shape["grp"] == 2 and mesh.shape["peer"] > 4
    return jax.shard_map(
        fused_device if fused else per_device,
        mesh=mesh,
        in_specs=(
            P(None, "peer", "grp", None, None, None),
            P(None, "peer", "grp", None, None, None),
            P("peer", None, "grp"),
            P("peer", None, "grp"),
            P("peer", "grp", None),
            P("peer", "grp"),
            P("peer", "grp", None),
            P("peer", None, "grp"),
            P("peer", None, "grp"),
            P("peer", "grp", None),
            P("peer", "grp"),
            P("peer", "grp", None),
        ),
        out_specs=(
            P("peer", None, "grp"),
            P("peer", None, "grp"),
            P("peer", "grp", None),
            P("peer", "grp"),
            P("peer", "grp", None),
            P("peer", "grp", None, None, None),
        ),
        check_vma=False,
    )
```
